32 devices in a mesh: group: 8 (over z, x), local: 4 (over y, core).
Axes of the slice: x: 2, y: 2, z: 4, core: 2. Of those that a mesh axis runs over, the one named last changes fastest.
Arguments:
- states_in: bfloat16 [32, 7168], P(('group', 'local')), may hold values from -24 to 24
- queries: bfloat16 [32, 128, 576], P(('group', 'local')), may hold values from -320 to 320
- kv_cache: bfloat16 [32, 1024, 576], P(('group', 'local')), may hold values from -5 to 5
- kv_new: bfloat16 [32, 576], P(('group', 'local')), may hold values from -12 to 12
- lengths: int32 [32], P(('group', 'local')), may hold values from 2 to 1024, as said below
- w_uv: bfloat16 [128, 512, 128], P(('group', 'local')), may hold values from -1.5 to 1.5
- w_out: bfloat16 [16384, 7168], P(('group', 'local')), may hold values from -0.046875 to 0.046875
- norm_gain: float32 [7168], replicated, may hold values from 0.25 to 1.75
- expert_ids: int32 [32, 8], P(('group', 'local')), may hold values from 0 to 23, as said below
- route_scores: float32 [32, 8], P(('group', 'local')), may hold values from 0.05 to 1
- w_gate: bfloat16 [24, 7168, 1024], P('group', None, 'local'), may hold values from -0.0625 to 0.0625
- w_up: bfloat16 [24, 7168, 1024], P('group', None, 'local'), may hold values from -0.0625 to 0.0625
- w_down: bfloat16 [24, 1024, 7168], P('group', 'local'), may hold values from -0.1875 to 0.1875
Outputs:
- residual: bfloat16 [32, 7168], P(('group', 'local'))
- layer_out: bfloat16 [32, 7168], P(('group', 'local'))
The draws below stay inside these ranges and needn't reach their ends.
Inputs may be any that keep to these rules, and one draw needn't show every extreme that they name: Each request attends to the first lengths entries of its cache and to its new token; some request has all 1024. `expert_ids`: each row names 8 different experts, all within at most 4 groups, where group g holds experts g * 3 to g * 3 + 2.
All inputs are finite; a program needn't handle non-finite values.
Results may differ from the reference program's by a relative error of at most 0.015.
Values may be sent and summed in bfloat16 or wider, within the bound.
A program may use at most 128 MiB of HBM per device.

```python
import math
import jax
import jax.numpy as jnp
from jax import lax

D = 7168
HEADS = 128
LAT = 512
ROPE = 64
VD = 128
EH = 1024
NGRP = 8
EXP_DEV = 3
TOPK = 8
TOPG = 4
CACHE = 1024
ROWS = 32
EXPERTS = 24
EXP_GRP = 3


def draw_kv_cache(key, part):
    own_key = jax.random.fold_in(key, 11)
    values = jnp.clip(jax.random.normal(own_key, (ROWS, CACHE, LAT + ROPE), jnp.float32), -5.0, 5.0)
    return values.astype(jnp.bfloat16)


def draw_queries(key, part):
    own_key = jax.random.fold_in(key, 13)
    values = jnp.clip(jax.random.normal(own_key, (ROWS, HEADS, LAT + ROPE), jnp.float32), -5.0, 5.0)
    return values.astype(jnp.bfloat16)


def draw_states_in(key, part):
    first_key, second_key, third_key = jax.random.split(key, 3)
    row_scale = jnp.exp(jax.random.uniform(second_key, (ROWS, 1), jnp.float32, math.log(0.4), math.log(2.5)))
    column_scale = jnp.exp(jax.random.uniform(third_key, (1, D), jnp.float32, math.log(0.3), math.log(3.0)))
    values = jnp.clip(jax.random.normal(first_key, (ROWS, D), jnp.float32), -4.0, 4.0) * row_scale * column_scale
    return jnp.clip(values, -24.0, 24.0).astype(jnp.bfloat16)


def draw_lengths(key, part):
    first_key, second_key, third_key = jax.random.split(key, 3)
    halvings = jax.random.randint(first_key, (ROWS,), 0, 4)
    longest = jnp.right_shift(jnp.full((ROWS,), CACHE, jnp.int32), halvings)
    trimmed = longest - jax.random.randint(second_key, (ROWS,), 0, CACHE // 16 + 1)
    chosen_row = jax.random.randint(third_key, (), 0, ROWS)
    return jnp.where(jnp.arange(ROWS) == chosen_row, CACHE, jnp.maximum(trimmed, 2)).astype(jnp.int32)


def draw_expert_ids(key, part):
    first_key, second_key, third_key = jax.random.split(key, 3)
    group_total = NGRP
    favour = jax.random.randint(first_key, (group_total,), 0, 3) * 131072
    group_score = (jax.random.randint(second_key, (ROWS, group_total), 0, 262144) + favour[None, :]) * 64 + jnp.arange(group_total, dtype=jnp.int32)[None, :]
    ignored, groups = lax.top_k(group_score, TOPG)
    candidates = TOPG * EXP_GRP
    pick_score = jax.random.randint(third_key, (ROWS, candidates), 0, 262144) * 1024 + jnp.arange(candidates, dtype=jnp.int32)[None, :]
    ignored_too, picks = lax.top_k(pick_score, TOPK)
    group_of = jnp.take_along_axis(groups, picks // EXP_GRP, axis=1)
    return (group_of * EXP_GRP + picks % EXP_GRP).astype(jnp.int32)


def level_of(stream_key, extent, cuts, smallest, high):
    factor_of = 1.0
    for axis_at, shards_of in cuts:
        heights = jax.random.uniform(jax.random.fold_in(jax.random.fold_in(stream_key, 6), axis_at), (shards_of,), jnp.float32, smallest / len(cuts), high / len(cuts))
        factor_of = factor_of * jnp.repeat(jnp.exp(heights), extent[axis_at] // shards_of).reshape((-1,) + (1,) * (len(extent) - 1 - axis_at))
    return factor_of


def noise(key, dims, width, limit, cuts=(), kind=jnp.bfloat16):
    gain = level_of(key, dims, cuts, -0.22, 0.18) if cuts else 1.0
    result = jax.random.normal(key, dims, jnp.float32) * width * gain
    return jnp.minimum(jnp.maximum(result, -limit), limit).astype(kind)


def setup_inputs(seed: int = 0) -> dict:
    key_of = jax.random.split(jax.random.key(seed), 14)
    states_in = draw_states_in(jax.random.fold_in(key_of[13], 71), 0)
    queries = draw_queries(jax.random.fold_in(key_of[13], 71), 0)
    kv_cache = draw_kv_cache(jax.random.fold_in(key_of[13], 71), 0)
    kv_new = noise(key_of[3], (ROWS, LAT + ROPE), 2.0, 12.0, ((0, 32),))
    lengths = draw_lengths(jax.random.fold_in(key_of[13], 71), 0)
    w_uv = noise(key_of[5], (HEADS, LAT, VD), 0.25, 1.5, ((0, 32),))
    w_out = noise(key_of[6], (HEADS * VD, D), (HEADS * VD) ** -0.5, 0.046875, ((0, 32),))
    norm_gain = jnp.clip(1.0 + 0.15 * jax.random.normal(key_of[7], (D,), jnp.float32), 0.25, 1.75)
    expert_ids = draw_expert_ids(jax.random.fold_in(key_of[13], 71), 0)
    route_scores = jnp.clip(jnp.exp(math.log(1.0) - 2.9957323 * jax.random.uniform(key_of[9], (ROWS, TOPK), jnp.float32) ** level_of(key_of[9], (ROWS, TOPK), ((0, 32),), -0.2, 0.2)), 0.05, 1.0)
    w_gate = noise(key_of[10], (EXPERTS, D, EH), D ** -0.5, 0.0625, ((0, 8), (2, 4)))
    w_up = noise(key_of[11], (EXPERTS, D, EH), D ** -0.5, 0.0625, ((0, 8), (2, 4)))
    w_down = noise(key_of[12], (EXPERTS, EH, D), EH ** -0.5, 0.1875, ((0, 8), (1, 4)))
    return {"states_in": states_in, "queries": queries, "kv_cache": kv_cache, "kv_new": kv_new, "lengths": lengths, "w_uv": w_uv, "w_out": w_out, "norm_gain": norm_gain, "expert_ids": expert_ids, "route_scores": route_scores, "w_gate": w_gate, "w_up": w_up, "w_down": w_down}


def attend_one(packed):
    query, cache_rows, newest, length = packed
    softmax_scale = (VD + ROPE) ** (-0.5)
    cached = jnp.dot(query, cache_rows.T, preferred_element_type=jnp.float32) * softmax_scale
    own_score = jnp.dot(query, newest, preferred_element_type=jnp.float32) * softmax_scale
    visible = (jnp.arange(CACHE, dtype=jnp.int32) < length)[None, :]
    highest = jnp.maximum(lax.optimization_barrier(jnp.max(jnp.where(visible, cached, -1e+30), axis=1)), own_score)
    weights_cached = jnp.exp(jnp.where(visible, cached - highest[:, None], -1e+30))
    weight_own = jnp.exp(own_score - highest)
    denominator = lax.optimization_barrier(jnp.sum(weights_cached, axis=1)) + weight_own
    probs_cached = (weights_cached / denominator[:, None]).astype(jnp.bfloat16)
    prob_own = (weight_own / denominator).astype(jnp.bfloat16)
    blended = jnp.dot(probs_cached, cache_rows[:, :LAT], preferred_element_type=jnp.float32)
    blended = blended + prob_own.astype(jnp.float32)[:, None] * newest[:LAT].astype(jnp.float32)[None, :]
    return blended.astype(jnp.bfloat16)

def reference(states_in, queries, kv_cache, kv_new, lengths, w_uv, w_out, norm_gain, expert_ids, route_scores, w_gate, w_up, w_down):
    latent_out = lax.map(attend_one, (queries, kv_cache, kv_new, lengths))
    values = jnp.einsum('rhl,hlv->rhv', latent_out.astype(jnp.float32), w_uv.astype(jnp.float32)).astype(jnp.bfloat16)
    attention = jnp.dot(values.reshape(ROWS, HEADS * VD), w_out, preferred_element_type=jnp.float32)
    residual = (states_in.astype(jnp.float32) + attention).astype(jnp.bfloat16)
    widened = residual.astype(jnp.float32)
    normed = (widened * lax.rsqrt(lax.optimization_barrier(jnp.mean(widened * widened, axis=1, keepdims=True)) + 1e-06) * norm_gain).astype(jnp.bfloat16)
    route_weights = (2.5 * route_scores / lax.optimization_barrier(jnp.sum(route_scores, axis=1, keepdims=True))).astype(jnp.bfloat16)
    chosen = expert_ids[:, :, None] == jnp.arange(EXPERTS, dtype=jnp.int32)[None, None, :]
    dense_weights = lax.optimization_barrier(jnp.sum(jnp.where(chosen, route_weights.astype(jnp.float32)[:, :, None], jnp.float32(0.0)), axis=1))
    block_total = EXPERTS // EXP_DEV
    by_block = dense_weights.reshape(ROWS, block_total, EXP_DEV)

    def one_block(carried, packed):
        index, gate_rows, up_rows, down_rows = packed
        weights = lax.dynamic_index_in_dim(by_block, index, axis=1, keepdims=False)
        part_sum = jnp.zeros((ROWS, D), jnp.float32)
        for expert in range(EXP_DEV):
            gate_proj = jnp.dot(normed, gate_rows[expert], preferred_element_type=jnp.float32)
            up_proj = jnp.dot(normed, up_rows[expert], preferred_element_type=jnp.float32)
            active = (jax.nn.silu(gate_proj) * up_proj).astype(jnp.bfloat16)
            output = jnp.dot(active, down_rows[expert], preferred_element_type=jnp.float32)
            part_sum = part_sum + weights[:, expert:expert + 1] * output
        rounded = lax.optimization_barrier(part_sum.astype(jnp.bfloat16))
        return (carried + rounded.astype(jnp.float32), None)
    indices = jnp.arange(block_total, dtype=jnp.int32)
    start_sum = jnp.zeros((ROWS, D), jnp.float32)
    expert_sum, unused = lax.scan(one_block, start_sum, (indices, w_gate.reshape(block_total, EXP_DEV, D, EH), w_up.reshape(block_total, EXP_DEV, D, EH), w_down.reshape(block_total, EXP_DEV, EH, D)))
    layer_out = (residual.astype(jnp.float32) + expert_sum).astype(jnp.bfloat16)
    return (residual, layer_out)
```

```python
import functools

import jax
import jax.numpy as jnp
from jax import lax
from jax.experimental import pallas as pl
from jax.experimental.pallas import tpu as pltpu
from jax.sharding import PartitionSpec as P

LAT = 512
ROPE = 64
VD = 128
CHUNKS = 2
SEG = 128
WIDE = 2
TILE = 16
MESH = pl.DeviceIdType.MESH
F32 = jnp.float32
BF16 = jnp.bfloat16


def kernel(
    dims,
    lengths,
    ids,
    scores,
    states,
    gain,
    kv_new,
    queries_hbm,
    cache_hbm,
    uv_hbm,
    out_hbm,
    gate_hbm,
    up_hbm,
    down_hbm,
    residual_out,
    layer_out,
    queries,
    cache,
    uv,
    wout,
    gate,
    up,
    down,
    lat32,
    lat_send,
    lat_got,
    stage,
    states32,
    gain32,
    res32,
    part,
    pair_got,
    pair_sum,
    row_got,
    rows,
    xmat,
    load_sem,
    lat_sem,
    pair_sem,
    scatter_sem,
    gather_sem,
    share_sem,
):
    group_count, local_count = dims
    n = group_count * local_count
    chips = n // 2
    group = lax.axis_index("group")
    local = lax.axis_index("local")
    me = group * local_count + local
    chip = me // 2
    core = lax.rem(me, 2)
    slot = core * chips + chip
    width = CHUNKS * SEG
    segs = states.shape[1] // width
    tall = stage.shape[0] // n
    heads = queries.shape[0]
    own_heads = uv.shape[0]
    per_head = lat32.shape[0] // heads
    lat_rows = own_heads * per_head
    experts, hidden = gate.shape[0], gate.shape[2]

    def device(index):
        return (index // local_count, lax.rem(index, local_count))

    partner = device(chip * 2 + 1 - core)

    first = [
        pltpu.make_async_copy(queries_hbm.at[0], queries, load_sem.at[0]),
        pltpu.make_async_copy(cache_hbm.at[0], cache, load_sem.at[1]),
    ]
    for copy in first:
        copy.start()
    barrier = pltpu.get_barrier_semaphore()

    def greet(k, carry):
        pl.semaphore_signal(
            barrier, inc=1, device_id=device(lax.rem(me + k, n)), device_id_type=MESH
        )
        return carry

    lax.fori_loop(1, n, greet, 0)

    load_uv = pltpu.make_async_copy(uv_hbm, uv, load_sem.at[2])
    load_out = pltpu.make_async_copy(out_hbm, wout, load_sem.at[3])
    load_gate = pltpu.make_async_copy(gate_hbm, gate, load_sem.at[4])
    load_up = pltpu.make_async_copy(up_hbm, up, load_sem.at[5])
    load_down = [
        pltpu.make_async_copy(
            down_hbm.at[e], down.at[pl.ds(e * hidden, hidden)], load_sem.at[6 + e]
        )
        for e in range(experts)
    ]

    states32[...] = jnp.zeros_like(states32)
    gain32[...] = jnp.zeros_like(gain32)
    stage[...] = jnp.zeros_like(stage)
    lat32[...] = jnp.zeros_like(lat32)
    for c in range(CHUNKS):
        for s in range(segs):
            at = (c * segs + s) * SEG
            states32[c, s : s + 1, :] = states[0:1, at : at + SEG].astype(F32)
            gain32[c, s : s + 1, :] = gain[0:1, at : at + SEG]

    lane = lax.broadcasted_iota(jnp.int32, (1, SEG), 1)
    score_sum = scores[0, 0]
    for k in range(1, scores.shape[1]):
        score_sum = score_sum + scores[0, k]
    dense = jnp.zeros((1, SEG), F32)
    for k in range(scores.shape[1]):
        weight = (
            jnp.full((1, SEG), 2.5 * scores[0, k], F32) / jnp.full((1, SEG), score_sum, F32)
        ).astype(BF16).astype(F32)
        dense = dense + jnp.where(lane == ids[0, k], weight, 0.0)

    for copy in first:
        copy.wait()
    for copy in [load_uv, load_out, load_gate, load_up] + load_down:
        copy.start()

    scale = (VD + ROPE) ** (-0.5)
    new = kv_new[...].astype(F32)
    cached = (
        lax.dot_general(
            queries[...], cache[...], (((1,), (1,)), ((), ())), preferred_element_type=F32
        )
        * scale
    )
    own = jnp.sum(queries[...].astype(F32) * new, axis=1, keepdims=True) * scale
    visible = lax.broadcasted_iota(jnp.int32, cached.shape, 1) < lengths[0]
    cached = jnp.where(visible, cached, -1e30)
    highest = jnp.maximum(jnp.max(cached, axis=1, keepdims=True), own)
    exps = jnp.exp(cached - highest)
    own_exp = jnp.exp(own - highest)
    denominator = jnp.sum(exps, axis=1, keepdims=True) + own_exp
    probs = (exps / denominator).astype(BF16)
    prob_own = (own_exp / denominator).astype(BF16).astype(F32)
    latent = jnp.dot(probs, cache[:, :LAT], preferred_element_type=F32)
    latent = latent + prob_own * new[:, :LAT]
    for q in range(LAT // 128):
        lat32[pl.ds(q, heads, stride=per_head), :] = latent[:, q * 128 : (q + 1) * 128]
    lat_send[...] = lat32[...].astype(BF16).reshape(lat_send.shape)

    pl.semaphore_wait(barrier, n - 1)

    def send_latent(k, carry):
        to = lax.rem(me + k, n)
        pltpu.make_async_remote_copy(
            src_ref=lat_send.at[to],
            dst_ref=lat_got.at[slot],
            send_sem=lat_sem.at[0],
            recv_sem=lat_sem.at[1],
            device_id=device(to),
            device_id_type=MESH,
        ).start()
        return carry

    lax.fori_loop(1, n, send_latent, 0)
    lat_got[pl.ds(slot, 1)] = lat_send[pl.ds(me, 1)]
    load_uv.wait()
    others = lat_got.at[pl.ds(0, n - 1)]
    pltpu.make_async_copy(others, others, lat_sem.at[1]).wait()
    lat32[...] = lat_got[...].astype(F32).reshape(lat32.shape)
    values = []
    for h in range(own_heads):
        by_head = jnp.concatenate(
            [
                lat32[pl.ds(h * per_head + q, n, stride=lat_rows), :]
                for q in range(LAT // 128)
            ],
            axis=1,
        ).astype(BF16)
        values.append(jnp.dot(by_head, uv[h], preferred_element_type=F32).astype(BF16))
    values = jnp.concatenate(values, axis=1)

    def scatter_sums(left, weight, turn):
        shares = []
        for c in range(CHUNKS):
            for s in range(0, segs, WIDE):
                at = (c * segs + s) * SEG
                product = jnp.dot(
                    left, weight[:, at : at + WIDE * SEG], preferred_element_type=F32
                )
                for w in range(WIDE):
                    stage[pl.ds(s + w, n, stride=tall), :] = product[:, w * SEG : (w + 1) * SEG]
            part[turn, c] = stage[...].astype(BF16).reshape(part.shape[2:])
            share = pltpu.make_async_remote_copy(
                src_ref=part.at[turn, c, pl.ds((1 - core) * chips, chips)],
                dst_ref=pair_got.at[turn, c],
                send_sem=pair_sem.at[0, turn, c],
                recv_sem=pair_sem.at[1, turn, c],
                device_id=partner,
                device_id_type=MESH,
            )
            share.start()
            shares.append(share)
        for c in range(CHUNKS):
            shares[c].wait()
            pair_sum[turn, c] = (
                part[turn, c, pl.ds(core * chips, chips)].astype(F32)
                + pair_got[turn, c].astype(F32)
            ).astype(BF16)

            def send_sum(k, carry):
                to = lax.rem(chip + k, chips)
                pltpu.make_async_remote_copy(
                    src_ref=pair_sum.at[turn, c, to],
                    dst_ref=row_got.at[turn, c, chip],
                    send_sem=scatter_sem.at[0, turn, c],
                    recv_sem=scatter_sem.at[1, turn, c],
                    device_id=device(to * 2 + core),
                    device_id_type=MESH,
                ).start()
                return carry

            lax.fori_loop(1, chips, send_sum, 0)
            row_got[turn, c, pl.ds(chip, 1)] = pair_sum[turn, c, pl.ds(chip, 1)]
        sums = []
        for c in range(CHUNKS):
            got = row_got.at[turn, c, pl.ds(0, chips - 1)]
            pltpu.make_async_copy(got, got, scatter_sem.at[1, turn, c]).wait()
            sums.append(jnp.sum(row_got[turn, c].astype(F32), axis=0))
        return sums

    load_out.wait()
    attention = scatter_sums(values, wout, 0)
    square = jnp.zeros((1, 1), F32)
    for c in range(CHUNKS):
        row = (states32[c] + attention[c]).astype(BF16).astype(F32)
        res32[c] = row
        square = square + jnp.sum(
            jnp.sum(row * row, axis=1, keepdims=True), axis=0, keepdims=True
        )
    factor = lax.rsqrt(square / states.shape[1] + 1e-6)
    for c in range(CHUNKS):
        normed = res32[c] * factor * gain32[c]
        if c == 0:
            at_row = lax.broadcasted_iota(jnp.int32, normed.shape, 0)
            normed = jnp.where(at_row == segs, dense, normed)
        rows[c, pl.ds(slot, 1)] = normed.astype(BF16)[None]

        def send_row(k, carry):
            to = lax.rem(chip + k, chips)
            pltpu.make_async_remote_copy(
                src_ref=rows.at[c, slot],
                dst_ref=rows.at[c, slot],
                send_sem=gather_sem.at[0, c],
                recv_sem=gather_sem.at[1, c],
                device_id=device(to * 2 + core),
                device_id_type=MESH,
            ).start()
            return carry

        lax.fori_loop(1, chips, send_row, 0)
    for c in range(CHUNKS):
        for s in range(segs):
            at = (c * segs + s) * SEG
            residual_out[0:1, at : at + SEG] = res32[c, s : s + 1, :].astype(BF16)
    shares = []
    for c in range(CHUNKS):
        got = rows.at[c, pl.ds(0, chips - 1)]
        pltpu.make_async_copy(got, got, gather_sem.at[1, c]).wait()
        mine = rows.at[c, pl.ds(core * chips, chips)]
        share = pltpu.make_async_remote_copy(
            src_ref=mine,
            dst_ref=mine,
            send_sem=share_sem.at[0, c],
            recv_sem=share_sem.at[1, c],
            device_id=partner,
            device_id_type=MESH,
        )
        share.start()
        shares.append(share)

    load_gate.wait()
    load_up.wait()
    gates = [None] * experts
    ups = [None] * experts
    weights = []
    deep = segs * SEG
    for c in range(CHUNKS):
        shares[c].wait()
        stage[...] = rows[c].astype(F32).reshape(stage.shape)
        for s in range(segs):
            xmat[:, s * SEG : (s + 1) * SEG] = stage[pl.ds(s, n, stride=tall), :].astype(BF16)
        if c == 0:
            table = stage[pl.ds(segs, n, stride=tall), :]
            lanes = lax.broadcasted_iota(jnp.int32, table.shape, 1)
            for e in range(experts):
                weights.append(
                    jnp.sum(
                        jnp.where(lanes == group * experts + e, table, 0.0),
                        axis=1,
                        keepdims=True,
                    )
                )
        left = xmat[...]
        for e in range(experts):
            gate_part = jnp.dot(
                left, gate[e, c * deep : (c + 1) * deep, :], preferred_element_type=F32
            )
            up_part = jnp.dot(
                left, up[e, c * deep : (c + 1) * deep, :], preferred_element_type=F32
            )
            gates[e] = gate_part if c == 0 else gates[e] + gate_part
            ups[e] = up_part if c == 0 else ups[e] + up_part
    active = jnp.concatenate(
        [
            (gates[e] / (1.0 + jnp.exp(-gates[e])) * ups[e] * weights[e]).astype(BF16)
            for e in range(experts)
        ],
        axis=1,
    )
    for copy in load_down:
        copy.wait()
    expert_sum = scatter_sums(active, down, 1)
    for c in range(CHUNKS):
        total = (res32[c] + expert_sum[c]).astype(BF16).astype(F32)
        res32[c] = total
        for s in range(segs):
            at = (c * segs + s) * SEG
            layer_out[0:1, at : at + SEG] = res32[c, s : s + 1, :].astype(BF16)

    sent = lat_send.at[pl.ds(0, n - 1)]
    pltpu.make_async_copy(sent, sent, lat_sem.at[0]).wait()
    for c in range(CHUNKS):
        sent = rows.at[c, pl.ds(0, chips - 1)]
        pltpu.make_async_copy(sent, sent, gather_sem.at[0, c]).wait()
        for turn in range(2):
            sent = pair_sum.at[turn, c, pl.ds(0, chips - 1)]
            pltpu.make_async_copy(sent, sent, scatter_sem.at[0, turn, c]).wait()


def body(
    group_count,
    local_count,
    states_in,
    queries,
    kv_cache,
    kv_new,
    lengths,
    w_uv,
    w_out,
    norm_gain,
    expert_ids,
    route_scores,
    w_gate,
    w_up,
    w_down,
):
    n = group_count * local_count
    chips = n // 2
    d = states_in.shape[1]
    heads, q_width = queries.shape[1:]
    cache_len = kv_cache.shape[1]
    own_heads = w_uv.shape[0]
    experts, _, hidden = w_gate.shape
    segs = d // (CHUNKS * SEG)
    tall = -(-(segs + 1) // TILE) * TILE
    per_head = max(LAT // 128, TILE // own_heads)
    lat_rows = own_heads * per_head
    smem = pl.BlockSpec(memory_space=pltpu.SMEM)
    vmem = pl.BlockSpec(memory_space=pltpu.VMEM)
    hbm = pl.BlockSpec(memory_space=pl.ANY)
    row = jax.ShapeDtypeStruct((1, d), BF16)
    return pl.pallas_call(
        functools.partial(kernel, (group_count, local_count)),
        out_shape=(row, row),
        in_specs=[smem] * 3 + [vmem] * 3 + [hbm] * 7,
        out_specs=(vmem, vmem),
        scratch_shapes=[
            pltpu.VMEM((heads, q_width), BF16),
            pltpu.VMEM((cache_len, q_width), BF16),
            pltpu.VMEM(w_uv.shape, BF16),
            pltpu.VMEM(w_out.shape, BF16),
            pltpu.VMEM(w_gate.shape, BF16),
            pltpu.VMEM(w_up.shape, BF16),
            pltpu.VMEM((experts * hidden, d), BF16),
            pltpu.VMEM((heads * per_head, 128), F32),
            pltpu.VMEM((n, lat_rows, 128), BF16),
            pltpu.VMEM((n, lat_rows, 128), BF16),
            pltpu.VMEM((n * tall, SEG), F32),
            pltpu.VMEM((CHUNKS, tall, SEG), F32),
            pltpu.VMEM((CHUNKS, tall, SEG), F32),
            pltpu.VMEM((CHUNKS, tall, SEG), F32),
            pltpu.VMEM((2, CHUNKS, n, tall, SEG), BF16),
            pltpu.VMEM((2, CHUNKS, chips, tall, SEG), BF16),
            pltpu.VMEM((2, CHUNKS, chips, tall, SEG), BF16),
            pltpu.VMEM((2, CHUNKS, chips, tall, SEG), BF16),
            pltpu.VMEM((CHUNKS, n, tall, SEG), BF16),
            pltpu.VMEM((n, segs * SEG), BF16),
            pltpu.SemaphoreType.DMA((6 + experts,)),
            pltpu.SemaphoreType.DMA((2,)),
            pltpu.SemaphoreType.DMA((2, 2, CHUNKS)),
            pltpu.SemaphoreType.DMA((2, 2, CHUNKS)),
            pltpu.SemaphoreType.DMA((2, CHUNKS)),
            pltpu.SemaphoreType.DMA((2, CHUNKS)),
        ],
        compiler_params=pltpu.CompilerParams(
            collective_id=0, has_side_effects=True, vmem_limit_bytes=60 * 1024 * 1024
        ),
    )(
        lengths,
        expert_ids,
        route_scores,
        states_in,
        norm_gain.reshape(1, d),
        kv_new,
        queries,
        kv_cache,
        w_uv,
        w_out,
        w_gate,
        w_up,
        w_down,
    )


def solution(mesh):
    in_specs = (
        P(("group", "local"), None),
        P(("group", "local"), None, None),
        P(("group", "local"), None, None),
        P(("group", "local"), None),
        P(("group", "local")),
        P(("group", "local"), None, None),
        P(("group", "local"), None),
        P(),
        P(("group", "local"), None),
        P(("group", "local"), None),
        P("group", None, "local"),
        P("group", None, "local"),
        P("group", "local", None),
    )
    out_specs = (P(("group", "local"), None), P(("group", "local"), None))
    sizes = (mesh.shape["group"], mesh.shape["local"])
    return jax.shard_map(
        functools.partial(body, *sizes),
        mesh=mesh,
        in_specs=in_specs,
        out_specs=out_specs,
        check_vma=False,
    )
```

```python
import functools

import jax
import jax.numpy as jnp
from jax import lax
from jax.experimental import pallas as pl
from jax.experimental.pallas import tpu as pltpu
from jax.sharding import PartitionSpec as P

LAT = 512
ROPE = 64
VD = 128
CHUNKS = 2
SEG = 128
WIDE = 2
TILE = 16
SLOW = 4
MESH = pl.DeviceIdType.MESH
F32 = jnp.float32
BF16 = jnp.bfloat16


def kernel(
    dims,
    lengths,
    ids,
    scores,
    states,
    gain,
    kv_new,
    queries_hbm,
    cache_hbm,
    uv_hbm,
    out_hbm,
    gate_hbm,
    up_hbm,
    down_hbm,
    final,
    queries,
    cache,
    uv,
    wout,
    gate,
    up,
    down,
    lat32,
    lat_send,
    lat_got,
    stage,
    states32,
    gain32,
    res32,
    part,
    pair_got,
    pair_sum,
    plane_got,
    plane_sum,
    row_got,
    rows,
    xmat,
    load_sem,
    lat_sem,
    pair_sem,
    plane_sem,
    scatter_sem,
    gather_sem,
    spread_sem,
    share_sem,
):
    group_count, local_count = dims
    n = group_count * local_count
    chips = n // 2
    group = lax.axis_index("group")
    local = lax.axis_index("local")
    me = group * local_count + local
    chip = me // 2
    core = lax.rem(me, 2)
    planes = SLOW if group_count % SLOW == 0 else 1
    plane = chips // planes
    far, near = chip // plane, lax.rem(chip, plane)
    slot = core * chips + near * planes + far
    width = CHUNKS * SEG
    segs = states.shape[1] // width
    tall = stage.shape[0] // n
    heads = queries.shape[1]
    own_heads = uv.shape[0]
    per_head = lat32.shape[0] // heads
    lat_rows = own_heads * per_head
    experts, hidden = gate.shape[0], gate.shape[2]

    def device(index):
        return (index // local_count, lax.rem(index, local_count))

    def same_core(to_far, to_near):
        return device((to_far * plane + to_near) * 2 + core)

    partner = device(chip * 2 + 1 - core)

    first = [
        pltpu.make_async_copy(queries_hbm.at[0], queries, load_sem.at[0]),
        pltpu.make_async_copy(cache_hbm.at[0], cache, load_sem.at[1]),
    ]
    for copy in first:
        copy.start()
    barrier = pltpu.get_barrier_semaphore()

    def greet(k, carry):
        pl.semaphore_signal(
            barrier, inc=1, device_id=device(lax.rem(me + k, n)), device_id_type=MESH
        )
        return carry

    lax.fori_loop(1, n, greet, 0)

    load_uv = pltpu.make_async_copy(uv_hbm, uv, load_sem.at[2])
    load_out = pltpu.make_async_copy(out_hbm, wout, load_sem.at[3])
    load_gate = pltpu.make_async_copy(gate_hbm, gate, load_sem.at[4])
    load_up = pltpu.make_async_copy(up_hbm, up, load_sem.at[5])
    load_down = [
        pltpu.make_async_copy(
            down_hbm.at[e], down.at[pl.ds(e * hidden, hidden)], load_sem.at[6 + e]
        )
        for e in range(experts)
    ]

    states32[...] = jnp.zeros_like(states32)
    gain32[...] = jnp.zeros_like(gain32)
    stage[...] = jnp.zeros_like(stage)
    lat32[...] = jnp.zeros_like(lat32)
    for c in range(CHUNKS):
        for s in range(segs):
            at = (c * segs + s) * SEG
            states32[c, s : s + 1, :] = states[0:1, at : at + SEG].astype(F32)
            gain32[c, s : s + 1, :] = gain[0:1, at : at + SEG]

    lane = lax.broadcasted_iota(jnp.int32, (1, SEG), 1)
    score_sum = scores[0, 0]
    for k in range(1, scores.shape[1]):
        score_sum = score_sum + scores[0, k]
    dense = jnp.zeros((1, SEG), F32)
    for k in range(scores.shape[1]):
        weight = (
            jnp.full((1, SEG), 2.5 * scores[0, k], F32) / jnp.full((1, SEG), score_sum, F32)
        ).astype(BF16).astype(F32)
        dense = dense + jnp.where(lane == ids[0, k], weight, 0.0)

    for copy in first:
        copy.wait()
    for copy in [load_uv, load_out, load_gate, load_up] + load_down:
        copy.start()

    scale = (VD + ROPE) ** (-0.5)
    new = kv_new[...].astype(F32)
    cached = (
        lax.dot_general(
            queries[...], cache[...], (((0,), (0,)), ((), ())), preferred_element_type=F32
        )
        * scale
    )
    own = (
        lax.dot_general(
            queries[...], kv_new[...], (((0,), (1,)), ((), ())), preferred_element_type=F32
        )
        * scale
    )
    visible = lax.broadcasted_iota(jnp.int32, cached.shape, 1) < lengths[0]
    cached = jnp.where(visible, cached, -1e30)
    highest = jnp.maximum(jnp.max(cached, axis=1, keepdims=True), own)
    exps = jnp.exp(cached - highest)
    own_exp = jnp.exp(own - highest)
    denominator = jnp.sum(exps, axis=1, keepdims=True) + own_exp
    probs = (exps * (1.0 / denominator)).astype(BF16)
    prob_own = (own_exp / denominator).astype(BF16).astype(F32)
    latent = lax.dot_general(
        probs, cache[:LAT, :], (((1,), (1,)), ((), ())), preferred_element_type=F32
    )
    latent = latent + prob_own * new[:, :LAT]
    for q in range(LAT // 128):
        lat32[pl.ds(q, heads, stride=per_head), :] = latent[:, q * 128 : (q + 1) * 128]
    lat_send[...] = lat32[...].astype(BF16).reshape(lat_send.shape)

    pl.semaphore_wait(barrier, n - 1)

    def send_latent(k, carry):
        to = lax.rem(me + k, n)
        pltpu.make_async_remote_copy(
            src_ref=lat_send.at[to],
            dst_ref=lat_got.at[slot],
            send_sem=lat_sem.at[0],
            recv_sem=lat_sem.at[1],
            device_id=device(to),
            device_id_type=MESH,
        ).start()
        return carry

    lax.fori_loop(1, n, send_latent, 0)
    lat_got[pl.ds(slot, 1)] = lat_send[pl.ds(me, 1)]
    load_uv.wait()
    others = lat_got.at[pl.ds(0, n - 1)]
    pltpu.make_async_copy(others, others, lat_sem.at[1]).wait()
    lat32[...] = lat_got[...].astype(F32).reshape(lat32.shape)
    values = []
    for h in range(own_heads):
        by_head = jnp.concatenate(
            [
                lat32[pl.ds(h * per_head + q, n, stride=lat_rows), :]
                for q in range(LAT // 128)
            ],
            axis=1,
        ).astype(BF16)
        values.append(jnp.dot(by_head, uv[h], preferred_element_type=F32).astype(BF16))
    values = jnp.concatenate(values, axis=1)

    def scatter_sums(left, weight, turn):
        shares = []

        def multiply(c):
            for s in range(0, segs, WIDE):
                at = (c * segs + s) * SEG
                product = jnp.dot(
                    left, weight[:, at : at + WIDE * SEG], preferred_element_type=F32
                )
                for w in range(WIDE):
                    stage[pl.ds(s + w, n, stride=tall), :] = product[:, w * SEG : (w + 1) * SEG]
            part[turn, c] = stage[...].astype(BF16).reshape(part.shape[2:])
            share = pltpu.make_async_remote_copy(
                src_ref=part.at[turn, c, pl.ds((1 - core) * chips, chips)],
                dst_ref=pair_got.at[turn, c],
                send_sem=pair_sem.at[0, turn, c],
                recv_sem=pair_sem.at[1, turn, c],
                device_id=partner,
                device_id_type=MESH,
            )
            share.start()
            shares.append(share)

        def add_pair(c):
            shares[c].wait()
            pair_sum[turn, c] = (
                (
                    part[turn, c, pl.ds(core * chips, chips)].astype(F32)
                    + pair_got[turn, c].astype(F32)
                )
                .astype(BF16)
                .reshape(pair_sum.shape[2:])
            )
            for k in range(1, plane):
                to = lax.rem(near + k, plane)
                pltpu.make_async_remote_copy(
                    src_ref=pair_sum.at[turn, c, to],
                    dst_ref=plane_got.at[turn, c, near],
                    send_sem=plane_sem.at[0, turn, c],
                    recv_sem=plane_sem.at[1, turn, c],
                    device_id=same_core(far, to),
                    device_id_type=MESH,
                ).start()
            plane_got[turn, c, pl.ds(near, 1)] = pair_sum[turn, c, pl.ds(near, 1)]

        def add_plane(c):
            got = plane_got.at[turn, c, pl.ds(0, plane - 1)]
            pltpu.make_async_copy(got, got, plane_sem.at[1, turn, c]).wait()
            plane_sum[turn, c] = jnp.sum(plane_got[turn, c].astype(F32), axis=0).astype(BF16)
            for k in range(1, planes):
                to = lax.rem(far + k, planes)
                pltpu.make_async_remote_copy(
                    src_ref=plane_sum.at[turn, c, to],
                    dst_ref=row_got.at[turn, c, far],
                    send_sem=scatter_sem.at[0, turn, c],
                    recv_sem=scatter_sem.at[1, turn, c],
                    device_id=same_core(to, near),
                    device_id_type=MESH,
                ).start()
            row_got[turn, c, pl.ds(far, 1)] = plane_sum[turn, c, pl.ds(far, 1)]

        for c in range(CHUNKS + 2):
            if c < CHUNKS:
                multiply(c)
            if 0 <= c - 1 < CHUNKS:
                add_pair(c - 1)
            if 0 <= c - 2:
                add_plane(c - 2)
        sums = []
        for c in range(CHUNKS):
            if planes > 1:
                got = row_got.at[turn, c, pl.ds(0, planes - 1)]
                pltpu.make_async_copy(got, got, scatter_sem.at[1, turn, c]).wait()
            sums.append(jnp.sum(row_got[turn, c].astype(F32), axis=0))
        return sums

    load_out.wait()
    attention = scatter_sums(values, wout, 0)
    square = jnp.zeros((1, 1), F32)
    for c in range(CHUNKS):
        row = (states32[c] + attention[c]).astype(BF16).astype(F32)
        res32[c] = row
        square = square + jnp.sum(
            jnp.sum(row * row, axis=1, keepdims=True), axis=0, keepdims=True
        )
    factor = lax.rsqrt(square / states.shape[1] + 1e-6)
    for c in range(CHUNKS):
        normed = res32[c] * factor * gain32[c]
        if c == 0:
            at_row = lax.broadcasted_iota(jnp.int32, normed.shape, 0)
            normed = jnp.where(at_row == segs, dense, normed)
        rows[c, pl.ds(slot, 1)] = normed.astype(BF16)[None]

        for k in range(1, planes):
            pltpu.make_async_remote_copy(
                src_ref=rows.at[c, slot],
                dst_ref=rows.at[c, slot],
                send_sem=gather_sem.at[0, c],
                recv_sem=gather_sem.at[1, c],
                device_id=same_core(lax.rem(far + k, planes), near),
                device_id_type=MESH,
            ).start()
    shares = []

    def spread(c):
        if planes > 1:
            got = rows.at[c, pl.ds(0, planes - 1)]
            pltpu.make_async_copy(got, got, gather_sem.at[1, c]).wait()
        mine = rows.at[c, pl.ds(core * chips + near * planes, planes)]
        for k in range(1, plane):
            pltpu.make_async_remote_copy(
                src_ref=mine,
                dst_ref=mine,
                send_sem=spread_sem.at[0, c],
                recv_sem=spread_sem.at[1, c],
                device_id=same_core(far, lax.rem(near + k, plane)),
                device_id_type=MESH,
            ).start()

    def hand_over(c):
        got = rows.at[c, pl.ds(0, chips - planes)]
        pltpu.make_async_copy(got, got, spread_sem.at[1, c]).wait()
        mine = rows.at[c, pl.ds(core * chips, chips)]
        share = pltpu.make_async_remote_copy(
            src_ref=mine,
            dst_ref=mine,
            send_sem=share_sem.at[0, c],
            recv_sem=share_sem.at[1, c],
            device_id=partner,
            device_id_type=MESH,
        )
        share.start()
        shares.append(share)

    for c in range(CHUNKS):
        spread(c)
        final[0, c] = res32[c]
    hand_over(0)

    load_gate.wait()
    load_up.wait()
    gates = [None] * experts
    ups = [None] * experts
    weights = []
    deep = segs * SEG
    for c in range(CHUNKS):
        shares[c].wait()
        stage[...] = rows[c].astype(F32).reshape(stage.shape)
        for s in range(segs):
            xmat[:, s * SEG : (s + 1) * SEG] = stage[pl.ds(s, n, stride=tall), :].astype(BF16)
        if c == 0:
            table = stage[pl.ds(segs, n, stride=tall), :]
            lanes = lax.broadcasted_iota(jnp.int32, table.shape, 1)
            for e in range(experts):
                weights.append(
                    jnp.sum(
                        jnp.where(lanes == group * experts + e, table, 0.0),
                        axis=1,
                        keepdims=True,
                    )
                )
        left = xmat[...]
        for e in range(experts):
            if e == 1 and c + 1 < CHUNKS:
                hand_over(c + 1)
            gate_part = jnp.dot(
                left, gate[e, c * deep : (c + 1) * deep, :], preferred_element_type=F32
            )
            up_part = jnp.dot(
                left, up[e, c * deep : (c + 1) * deep, :], preferred_element_type=F32
            )
            gates[e] = gate_part if c == 0 else gates[e] + gate_part
            ups[e] = up_part if c == 0 else ups[e] + up_part
    active = jnp.concatenate(
        [
            (gates[e] / (1.0 + jnp.exp(-gates[e])) * ups[e] * weights[e]).astype(BF16)
            for e in range(experts)
        ],
        axis=1,
    )
    for copy in load_down:
        copy.wait()
    expert_sum = scatter_sums(active, down, 1)
    for c in range(CHUNKS):
        final[1, c] = res32[c] + expert_sum[c]

    sent = lat_send.at[pl.ds(0, n - 1)]
    pltpu.make_async_copy(sent, sent, lat_sem.at[0]).wait()
    for c in range(CHUNKS):
        if planes > 1:
            sent = rows.at[c, pl.ds(0, planes - 1)]
            pltpu.make_async_copy(sent, sent, gather_sem.at[0, c]).wait()
        sent = rows.at[c, pl.ds(0, chips - planes)]
        pltpu.make_async_copy(sent, sent, spread_sem.at[0, c]).wait()
        for turn in range(2):
            sent = pair_sum.at[turn, c, pl.ds(0, plane - 1)]
            pltpu.make_async_copy(sent, sent, plane_sem.at[0, turn, c]).wait()
            if planes > 1:
                sent = plane_sum.at[turn, c, pl.ds(0, planes - 1)]
                pltpu.make_async_copy(sent, sent, scatter_sem.at[0, turn, c]).wait()


def write_rows(final, residual_out, layer_out):
    segs = residual_out.shape[1] // (CHUNKS * SEG)
    for which, out in enumerate((residual_out, layer_out)):
        for c in range(CHUNKS):
            for s in range(segs):
                at = (c * segs + s) * SEG
                out[0:1, at : at + SEG] = final[which, c, s : s + 1, :].astype(BF16)


def body(
    group_count,
    local_count,
    states_in,
    queries,
    kv_cache,
    kv_new,
    lengths,
    w_uv,
    w_out,
    norm_gain,
    expert_ids,
    route_scores,
    w_gate,
    w_up,
    w_down,
):
    n = group_count * local_count
    chips = n // 2
    d = states_in.shape[1]
    heads, q_width = queries.shape[1:]
    cache_len = kv_cache.shape[1]
    planes = SLOW if group_count % SLOW == 0 else 1
    plane = chips // planes
    own_heads = w_uv.shape[0]
    experts, _, hidden = w_gate.shape
    segs = d // (CHUNKS * SEG)
    tall = -(-(segs + 1) // TILE) * TILE
    per_head = max(LAT // 128, TILE // own_heads)
    lat_rows = own_heads * per_head
    smem = pl.BlockSpec(memory_space=pltpu.SMEM)
    vmem = pl.BlockSpec(memory_space=pltpu.VMEM)
    hbm = pl.BlockSpec(memory_space=pl.ANY)
    row = jax.ShapeDtypeStruct((1, d), BF16)
    final = pl.pallas_call(
        functools.partial(kernel, (group_count, local_count)),
        out_shape=jax.ShapeDtypeStruct((2, CHUNKS, tall, SEG), F32),
        in_specs=[smem] * 3 + [vmem] * 3 + [hbm] * 7,
        out_specs=vmem,
        scratch_shapes=[
            pltpu.VMEM((q_width, heads), BF16),
            pltpu.VMEM((q_width, cache_len), BF16),
            pltpu.VMEM(w_uv.shape, BF16),
            pltpu.VMEM(w_out.shape, BF16),
            pltpu.VMEM(w_gate.shape, BF16),
            pltpu.VMEM(w_up.shape, BF16),
            pltpu.VMEM((experts * hidden, d), BF16),
            pltpu.VMEM((heads * per_head, 128), F32),
            pltpu.VMEM((n, lat_rows, 128), BF16),
            pltpu.VMEM((n, lat_rows, 128), BF16),
            pltpu.VMEM((n * tall, SEG), F32),
            pltpu.VMEM((CHUNKS, tall, SEG), F32),
            pltpu.VMEM((CHUNKS, tall, SEG), F32),
            pltpu.VMEM((CHUNKS, tall, SEG), F32),
            pltpu.VMEM((2, CHUNKS, n, tall, SEG), BF16),
            pltpu.VMEM((2, CHUNKS, chips, tall, SEG), BF16),
            pltpu.VMEM((2, CHUNKS, plane, planes, tall, SEG), BF16),
            pltpu.VMEM((2, CHUNKS, plane, planes, tall, SEG), BF16),
            pltpu.VMEM((2, CHUNKS, planes, tall, SEG), BF16),
            pltpu.VMEM((2, CHUNKS, planes, tall, SEG), BF16),
            pltpu.VMEM((CHUNKS, n, tall, SEG), BF16),
            pltpu.VMEM((n, segs * SEG), BF16),
            pltpu.SemaphoreType.DMA((6 + experts,)),
            pltpu.SemaphoreType.DMA((2,)),
            pltpu.SemaphoreType.DMA((2, 2, CHUNKS)),
            pltpu.SemaphoreType.DMA((2, 2, CHUNKS)),
            pltpu.SemaphoreType.DMA((2, 2, CHUNKS)),
            pltpu.SemaphoreType.DMA((2, CHUNKS)),
            pltpu.SemaphoreType.DMA((2, CHUNKS)),
            pltpu.SemaphoreType.DMA((2, CHUNKS)),
        ],
        compiler_params=pltpu.CompilerParams(
            collective_id=0, has_side_effects=True, vmem_limit_bytes=60 * 1024 * 1024
        ),
    )(
        lengths,
        expert_ids,
        route_scores,
        states_in,
        norm_gain.reshape(1, d),
        kv_new,
        jnp.swapaxes(queries, 1, 2),
        jnp.swapaxes(kv_cache, 1, 2),
        w_uv,
        w_out,
        w_gate,
        w_up,
        w_down,
    )
    return pl.pallas_call(
        write_rows, out_shape=(row, row), in_specs=[vmem], out_specs=(vmem, vmem)
    )(final)


def solution(mesh):
    in_specs = (
        P(("group", "local"), None),
        P(("group", "local"), None, None),
        P(("group", "local"), None, None),
        P(("group", "local"), None),
        P(("group", "local")),
        P(("group", "local"), None, None),
        P(("group", "local"), None),
        P(),
        P(("group", "local"), None),
        P(("group", "local"), None),
        P("group", None, "local"),
        P("group", None, "local"),
        P("group", "local", None),
    )
    out_specs = (P(("group", "local"), None), P(("group", "local"), None))
    sizes = (mesh.shape["group"], mesh.shape["local"])
    return jax.shard_map(
        functools.partial(body, *sizes),
        mesh=mesh,
        in_specs=in_specs,
        out_specs=out_specs,
        check_vma=False,
    )
```

```python
import functools

import jax
import jax.numpy as jnp
from jax import lax
from jax.experimental import pallas as pl
from jax.experimental.pallas import tpu as pltpu
from jax.sharding import PartitionSpec as P

LAT = 512
ROPE = 64
VD = 128
CHUNKS = 2
SEG = 128
WIDE = 2
TILE = 16
PIECES = 4
SLOW = 4
MESH = pl.DeviceIdType.MESH
F32 = jnp.float32
BF16 = jnp.bfloat16


def kernel(
    dims,
    lengths,
    ids,
    scores,
    states,
    gain,
    kv_new,
    queries_hbm,
    cache_hbm,
    uv_hbm,
    out_hbm,
    gate_hbm,
    up_hbm,
    down_hbm,
    final,
    queries,
    cache,
    uv,
    wout,
    gate,
    up,
    down,
    lat32,
    lat_send,
    lat_got,
    stage,
    states32,
    gain32,
    res32,
    part,
    pair_got,
    pair_sum,
    plane_got,
    plane_sum,
    row_got,
    rows,
    xmat,
    load_sem,
    lat_sem,
    pair_sem,
    plane_sem,
    scatter_sem,
    gather_sem,
    spread_sem,
    share_sem,
):
    group_count, local_count = dims
    n = group_count * local_count
    chips = n // 2
    group = lax.axis_index("group")
    local = lax.axis_index("local")
    me = group * local_count + local
    chip = me // 2
    core = lax.rem(me, 2)
    planes = SLOW if group_count % SLOW == 0 else 1
    plane = chips // planes
    far, near = chip // plane, lax.rem(chip, plane)
    slot = core * chips + near * planes + far
    width = CHUNKS * SEG
    segs = states.shape[1] // width
    tall = stage.shape[0] // n
    heads = queries.shape[1]
    own_heads = uv.shape[0]
    per_head = lat32.shape[0] // heads
    lat_rows = own_heads * per_head
    experts, hidden = gate.shape[0], gate.shape[2]

    def device(index):
        return (index // local_count, lax.rem(index, local_count))

    def same_core(to_far, to_near):
        return device((to_far * plane + to_near) * 2 + core)

    partner = device(chip * 2 + 1 - core)

    first = [
        pltpu.make_async_copy(queries_hbm.at[0], queries, load_sem.at[0]),
        pltpu.make_async_copy(cache_hbm.at[0], cache, load_sem.at[1]),
    ]
    for copy in first:
        copy.start()
    barrier = pltpu.get_barrier_semaphore()

    def greet(k, carry):
        pl.semaphore_signal(
            barrier, inc=1, device_id=device(lax.rem(me + k, n)), device_id_type=MESH
        )
        return carry

    lax.fori_loop(1, n, greet, 0)

    load_uv = pltpu.make_async_copy(uv_hbm, uv, load_sem.at[2])
    block = wout.shape[0] // PIECES
    load_out = [
        pltpu.make_async_copy(
            out_hbm.at[pl.ds(i * block, block)],
            wout.at[pl.ds(i * block, block)],
            load_sem.at[3 + i],
        )
        for i in range(PIECES)
    ]
    deep = segs * SEG
    load_gate = []
    load_up = []
    load_down = []
    for c in range(CHUNKS):
        for e in range(experts):
            at = 3 + PIECES + (c * experts + e) * 3
            half = pl.ds(c * deep, deep)
            load_gate.append(
                pltpu.make_async_copy(
                    gate_hbm.at[e, half], gate.at[e, half], load_sem.at[at]
                )
            )
            load_up.append(
                pltpu.make_async_copy(up_hbm.at[e, half], up.at[e, half], load_sem.at[at + 1])
            )
            half_rows = hidden // CHUNKS
            load_down.append(
                pltpu.make_async_copy(
                    down_hbm.at[e, pl.ds(c * half_rows, half_rows)],
                    down.at[pl.ds(e * hidden + c * half_rows, half_rows)],
                    load_sem.at[at + 2],
                )
            )

    states32[...] = jnp.zeros_like(states32)
    gain32[...] = jnp.zeros_like(gain32)
    stage[...] = jnp.zeros_like(stage)
    lat32[...] = jnp.zeros_like(lat32)
    for c in range(CHUNKS):
        for s in range(segs):
            at = (c * segs + s) * SEG
            states32[c, s : s + 1, :] = states[0:1, at : at + SEG].astype(F32)
            gain32[c, s : s + 1, :] = gain[0:1, at : at + SEG]

    lane = lax.broadcasted_iota(jnp.int32, (1, SEG), 1)
    score_sum = scores[0, 0]
    for k in range(1, scores.shape[1]):
        score_sum = score_sum + scores[0, k]
    dense = jnp.zeros((1, SEG), F32)
    for k in range(scores.shape[1]):
        weight = (
            jnp.full((1, SEG), 2.5 * scores[0, k], F32) / jnp.full((1, SEG), score_sum, F32)
        ).astype(BF16).astype(F32)
        dense = dense + jnp.where(lane == ids[0, k], weight, 0.0)

    for copy in first:
        copy.wait()
    for copy in [load_uv] + load_out:
        copy.start()

    scale = (VD + ROPE) ** (-0.5)
    new = kv_new[...].astype(F32)
    cached = (
        lax.dot_general(
            queries[...], cache[...], (((0,), (0,)), ((), ())), preferred_element_type=F32
        )
        * scale
    )
    own = (
        lax.dot_general(
            queries[...], kv_new[...], (((0,), (1,)), ((), ())), preferred_element_type=F32
        )
        * scale
    )
    visible = lax.broadcasted_iota(jnp.int32, cached.shape, 1) < lengths[0]
    cached = jnp.where(visible, cached, -1e30)
    highest = jnp.maximum(jnp.max(cached, axis=1, keepdims=True), own)
    exps = jnp.exp(cached - highest)
    own_exp = jnp.exp(own - highest)
    denominator = jnp.sum(exps, axis=1, keepdims=True) + own_exp
    probs = (exps * (1.0 / denominator)).astype(BF16)
    prob_own = (own_exp / denominator).astype(BF16).astype(F32)
    for i in range(len(load_gate)):
        load_gate[i].start()
        load_up[i].start()
    latent = lax.dot_general(
        cache[:LAT, :], probs, (((1,), (1,)), ((), ())), preferred_element_type=F32
    ).T
    latent = latent + prob_own * new[:, :LAT]
    for q in range(LAT // 128):
        lat32[pl.ds(q, heads, stride=per_head), :] = latent[:, q * 128 : (q + 1) * 128]
    lat_send[...] = lat32[...].astype(BF16).reshape(lat_send.shape)

    pl.semaphore_wait(barrier, n - 1)

    def send_latent(k, carry):
        to = lax.rem(me + k, n)
        pltpu.make_async_remote_copy(
            src_ref=lat_send.at[to],
            dst_ref=lat_got.at[slot],
            send_sem=lat_sem.at[0],
            recv_sem=lat_sem.at[1],
            device_id=device(to),
            device_id_type=MESH,
        ).start()
        return carry

    lax.fori_loop(1, n, send_latent, 0)
    lat_got[pl.ds(slot, 1)] = lat_send[pl.ds(me, 1)]
    for copy in load_down:
        copy.start()
    load_uv.wait()
    others = lat_got.at[pl.ds(0, n - 1)]
    pltpu.make_async_copy(others, others, lat_sem.at[1]).wait()
    lat32[...] = lat_got[...].astype(F32).reshape(lat32.shape)
    values = []
    for h in range(own_heads):
        by_head = jnp.concatenate(
            [
                lat32[pl.ds(h * per_head + q, n, stride=lat_rows), :]
                for q in range(LAT // 128)
            ],
            axis=1,
        ).astype(BF16)
        values.append(jnp.dot(by_head, uv[h], preferred_element_type=F32).astype(BF16))
    values = jnp.concatenate(values, axis=1)

    def scatter_sums(left, weight, turn):
        shares = []

        def multiply(c):
            for s in range(0, segs, WIDE):
                at = (c * segs + s) * SEG
                product = jnp.dot(
                    left, weight[:, at : at + WIDE * SEG], preferred_element_type=F32
                )
                for w in range(WIDE):
                    stage[pl.ds(s + w, n, stride=tall), :] = product[:, w * SEG : (w + 1) * SEG]
            part[turn, c] = stage[...].astype(BF16).reshape(part.shape[2:])
            share = pltpu.make_async_remote_copy(
                src_ref=part.at[turn, c, pl.ds((1 - core) * chips, chips)],
                dst_ref=pair_got.at[turn, c],
                send_sem=pair_sem.at[0, turn, c],
                recv_sem=pair_sem.at[1, turn, c],
                device_id=partner,
                device_id_type=MESH,
            )
            share.start()
            shares.append(share)

        def add_pair(c):
            shares[c].wait()
            pair_sum[turn, c] = (
                (
                    part[turn, c, pl.ds(core * chips, chips)].astype(F32)
                    + pair_got[turn, c].astype(F32)
                )
                .astype(BF16)
                .reshape(pair_sum.shape[2:])
            )
            for k in range(1, plane):
                to = lax.rem(near + k, plane)
                pltpu.make_async_remote_copy(
                    src_ref=pair_sum.at[turn, c, to],
                    dst_ref=plane_got.at[turn, c, near],
                    send_sem=plane_sem.at[0, turn, c],
                    recv_sem=plane_sem.at[1, turn, c],
                    device_id=same_core(far, to),
                    device_id_type=MESH,
                ).start()
            plane_got[turn, c, pl.ds(near, 1)] = pair_sum[turn, c, pl.ds(near, 1)]

        def add_plane(c):
            got = plane_got.at[turn, c, pl.ds(0, plane - 1)]
            pltpu.make_async_copy(got, got, plane_sem.at[1, turn, c]).wait()
            plane_sum[turn, c] = jnp.sum(plane_got[turn, c].astype(F32), axis=0).astype(BF16)
            for k in range(1, planes):
                to = lax.rem(far + k, planes)
                pltpu.make_async_remote_copy(
                    src_ref=plane_sum.at[turn, c, to],
                    dst_ref=row_got.at[turn, c, far],
                    send_sem=scatter_sem.at[0, turn, c],
                    recv_sem=scatter_sem.at[1, turn, c],
                    device_id=same_core(to, near),
                    device_id_type=MESH,
                ).start()
            row_got[turn, c, pl.ds(far, 1)] = plane_sum[turn, c, pl.ds(far, 1)]

        for c in range(CHUNKS + 2):
            if c < CHUNKS:
                multiply(c)
            if 0 <= c - 1 < CHUNKS:
                add_pair(c - 1)
            if 0 <= c - 2:
                add_plane(c - 2)
        sums = []
        for c in range(CHUNKS):
            if planes > 1:
                got = row_got.at[turn, c, pl.ds(0, planes - 1)]
                pltpu.make_async_copy(got, got, scatter_sem.at[1, turn, c]).wait()
            sums.append(jnp.sum(row_got[turn, c].astype(F32), axis=0))
        return sums

    for copy in load_out:
        copy.wait()
    attention = scatter_sums(values, wout, 0)
    square = jnp.zeros((1, 1), F32)
    for c in range(CHUNKS):
        row = (states32[c] + attention[c]).astype(BF16).astype(F32)
        res32[c] = row
        square = square + jnp.sum(
            jnp.sum(row * row, axis=1, keepdims=True), axis=0, keepdims=True
        )
    factor = lax.rsqrt(square / states.shape[1] + 1e-6)
    for c in range(CHUNKS):
        normed = res32[c] * factor * gain32[c]
        if c == 0:
            at_row = lax.broadcasted_iota(jnp.int32, normed.shape, 0)
            normed = jnp.where(at_row == segs, dense, normed)
        rows[c, pl.ds(slot, 1)] = normed.astype(BF16)[None]

        for k in range(1, planes):
            pltpu.make_async_remote_copy(
                src_ref=rows.at[c, slot],
                dst_ref=rows.at[c, slot],
                send_sem=gather_sem.at[0, c],
                recv_sem=gather_sem.at[1, c],
                device_id=same_core(lax.rem(far + k, planes), near),
                device_id_type=MESH,
            ).start()
    shares = []

    def spread(c):
        if planes > 1:
            got = rows.at[c, pl.ds(0, planes - 1)]
            pltpu.make_async_copy(got, got, gather_sem.at[1, c]).wait()
        mine = rows.at[c, pl.ds(core * chips + near * planes, planes)]
        for k in range(1, plane):
            pltpu.make_async_remote_copy(
                src_ref=mine,
                dst_ref=mine,
                send_sem=spread_sem.at[0, c],
                recv_sem=spread_sem.at[1, c],
                device_id=same_core(far, lax.rem(near + k, plane)),
                device_id_type=MESH,
            ).start()

    def hand_over(c):
        got = rows.at[c, pl.ds(0, chips - planes)]
        pltpu.make_async_copy(got, got, spread_sem.at[1, c]).wait()
        mine = rows.at[c, pl.ds(core * chips, chips)]
        share = pltpu.make_async_remote_copy(
            src_ref=mine,
            dst_ref=mine,
            send_sem=share_sem.at[0, c],
            recv_sem=share_sem.at[1, c],
            device_id=partner,
            device_id_type=MESH,
        )
        share.start()
        shares.append(share)

    for c in range(CHUNKS):
        spread(c)
        final[0, c] = res32[c]
    hand_over(0)

    gates = [None] * experts
    ups = [None] * experts
    weights = []
    for c in range(CHUNKS):
        shares[c].wait()
        stage[...] = rows[c].astype(F32).reshape(stage.shape)
        for s in range(segs):
            xmat[:, s * SEG : (s + 1) * SEG] = stage[pl.ds(s, n, stride=tall), :].astype(BF16)
        if c == 0:
            table = stage[pl.ds(segs, n, stride=tall), :]
            lanes = lax.broadcasted_iota(jnp.int32, table.shape, 1)
            for e in range(experts):
                weights.append(
                    jnp.sum(
                        jnp.where(lanes == group * experts + e, table, 0.0),
                        axis=1,
                        keepdims=True,
                    )
                )
        left = xmat[...]
        for e in range(experts):
            if e == 1 and c + 1 < CHUNKS:
                hand_over(c + 1)
            load_gate[c * experts + e].wait()
            load_up[c * experts + e].wait()
            gate_part = jnp.dot(
                left, gate[e, c * deep : (c + 1) * deep, :], preferred_element_type=F32
            )
            up_part = jnp.dot(
                left, up[e, c * deep : (c + 1) * deep, :], preferred_element_type=F32
            )
            gates[e] = gate_part if c == 0 else gates[e] + gate_part
            ups[e] = up_part if c == 0 else ups[e] + up_part
    active = jnp.concatenate(
        [
            (gates[e] / (1.0 + jnp.exp(-gates[e])) * ups[e] * weights[e]).astype(BF16)
            for e in range(experts)
        ],
        axis=1,
    )
    for copy in load_down:
        copy.wait()
    expert_sum = scatter_sums(active, down, 1)
    for c in range(CHUNKS):
        final[1, c] = res32[c] + expert_sum[c]

    sent = lat_send.at[pl.ds(0, n - 1)]
    pltpu.make_async_copy(sent, sent, lat_sem.at[0]).wait()
    for c in range(CHUNKS):
        if planes > 1:
            sent = rows.at[c, pl.ds(0, planes - 1)]
            pltpu.make_async_copy(sent, sent, gather_sem.at[0, c]).wait()
        sent = rows.at[c, pl.ds(0, chips - planes)]
        pltpu.make_async_copy(sent, sent, spread_sem.at[0, c]).wait()
        for turn in range(2):
            sent = pair_sum.at[turn, c, pl.ds(0, plane - 1)]
            pltpu.make_async_copy(sent, sent, plane_sem.at[0, turn, c]).wait()
            if planes > 1:
                sent = plane_sum.at[turn, c, pl.ds(0, planes - 1)]
                pltpu.make_async_copy(sent, sent, scatter_sem.at[0, turn, c]).wait()


def write_rows(final, residual_out, layer_out):
    segs = residual_out.shape[1] // (CHUNKS * SEG)
    for which, out in enumerate((residual_out, layer_out)):
        for c in range(CHUNKS):
            for s in range(segs):
                at = (c * segs + s) * SEG
                out[0:1, at : at + SEG] = final[which, c, s : s + 1, :].astype(BF16)


def body(
    group_count,
    local_count,
    states_in,
    queries,
    kv_cache,
    kv_new,
    lengths,
    w_uv,
    w_out,
    norm_gain,
    expert_ids,
    route_scores,
    w_gate,
    w_up,
    w_down,
):
    n = group_count * local_count
    chips = n // 2
    d = states_in.shape[1]
    heads, q_width = queries.shape[1:]
    cache_len = kv_cache.shape[1]
    planes = SLOW if group_count % SLOW == 0 else 1
    plane = chips // planes
    own_heads = w_uv.shape[0]
    experts, _, hidden = w_gate.shape
    segs = d // (CHUNKS * SEG)
    tall = -(-(segs + 1) // TILE) * TILE
    per_head = max(LAT // 128, TILE // own_heads)
    lat_rows = own_heads * per_head
    smem = pl.BlockSpec(memory_space=pltpu.SMEM)
    vmem = pl.BlockSpec(memory_space=pltpu.VMEM)
    hbm = pl.BlockSpec(memory_space=pl.ANY)
    row = jax.ShapeDtypeStruct((1, d), BF16)
    final = pl.pallas_call(
        functools.partial(kernel, (group_count, local_count)),
        out_shape=jax.ShapeDtypeStruct((2, CHUNKS, tall, SEG), F32),
        in_specs=[smem] * 3 + [vmem] * 3 + [hbm] * 7,
        out_specs=vmem,
        scratch_shapes=[
            pltpu.VMEM((q_width, heads), BF16),
            pltpu.VMEM((q_width, cache_len), BF16),
            pltpu.VMEM(w_uv.shape, BF16),
            pltpu.VMEM(w_out.shape, BF16),
            pltpu.VMEM(w_gate.shape, BF16),
            pltpu.VMEM(w_up.shape, BF16),
            pltpu.VMEM((experts * hidden, d), BF16),
            pltpu.VMEM((heads * per_head, 128), F32),
            pltpu.VMEM((n, lat_rows, 128), BF16),
            pltpu.VMEM((n, lat_rows, 128), BF16),
            pltpu.VMEM((n * tall, SEG), F32),
            pltpu.VMEM((CHUNKS, tall, SEG), F32),
            pltpu.VMEM((CHUNKS, tall, SEG), F32),
            pltpu.VMEM((CHUNKS, tall, SEG), F32),
            pltpu.VMEM((2, CHUNKS, n, tall, SEG), BF16),
            pltpu.VMEM((2, CHUNKS, chips, tall, SEG), BF16),
            pltpu.VMEM((2, CHUNKS, plane, planes, tall, SEG), BF16),
            pltpu.VMEM((2, CHUNKS, plane, planes, tall, SEG), BF16),
            pltpu.VMEM((2, CHUNKS, planes, tall, SEG), BF16),
            pltpu.VMEM((2, CHUNKS, planes, tall, SEG), BF16),
            pltpu.VMEM((CHUNKS, n, tall, SEG), BF16),
            pltpu.VMEM((n, segs * SEG), BF16),
            pltpu.SemaphoreType.DMA((3 + PIECES + 3 * CHUNKS * experts,)),
            pltpu.SemaphoreType.DMA((2,)),
            pltpu.SemaphoreType.DMA((2, 2, CHUNKS)),
            pltpu.SemaphoreType.DMA((2, 2, CHUNKS)),
            pltpu.SemaphoreType.DMA((2, 2, CHUNKS)),
            pltpu.SemaphoreType.DMA((2, CHUNKS)),
            pltpu.SemaphoreType.DMA((2, CHUNKS)),
            pltpu.SemaphoreType.DMA((2, CHUNKS)),
        ],
        compiler_params=pltpu.CompilerParams(
            collective_id=0, has_side_effects=True, vmem_limit_bytes=60 * 1024 * 1024
        ),
    )(
        lengths,
        expert_ids,
        route_scores,
        states_in,
        norm_gain.reshape(1, d),
        kv_new,
        jnp.swapaxes(queries, 1, 2),
        jnp.swapaxes(kv_cache, 1, 2),
        w_uv,
        w_out,
        w_gate,
        w_up,
        w_down,
    )
    return pl.pallas_call(
        write_rows, out_shape=(row, row), in_specs=[vmem], out_specs=(vmem, vmem)
    )(final)


def solution(mesh):
    in_specs = (
        P(("group", "local"), None),
        P(("group", "local"), None, None),
        P(("group", "local"), None, None),
        P(("group", "local"), None),
        P(("group", "local")),
        P(("group", "local"), None, None),
        P(("group", "local"), None),
        P(),
        P(("group", "local"), None),
        P(("group", "local"), None),
        P("group", None, "local"),
        P("group", None, "local"),
        P("group", "local", None),
    )
    out_specs = (P(("group", "local"), None), P(("group", "local"), None))
    sizes = (mesh.shape["group"], mesh.shape["local"])
    return jax.shard_map(
        functools.partial(body, *sizes),
        mesh=mesh,
        in_specs=in_specs,
        out_specs=out_specs,
        check_vma=False,
    )
```

```python
import functools

import jax
import jax.numpy as jnp
from jax import lax
from jax.experimental import pallas as pl
from jax.experimental.pallas import tpu as pltpu
from jax.sharding import PartitionSpec as P

LAT = 512
ROPE = 64
VD = 128
CHUNKS = 2
SEG = 128
WIDE = 2
TILE = 16
PIECES = 4
SLOW = 1
MESH = pl.DeviceIdType.MESH
F32 = jnp.float32
BF16 = jnp.bfloat16


def kernel(
    dims,
    lengths,
    ids_hbm,
    scores_hbm,
    states_hbm,
    gain_hbm,
    new_hbm,
    queries_hbm,
    cache_hbm,
    uv_hbm,
    out_hbm,
    gate_hbm,
    up_hbm,
    down_hbm,
    final,
    ids,
    scores,
    states,
    gain,
    kv_new,
    queries,
    cache,
    uv,
    wout,
    gate,
    up,
    down,
    lat32,
    lat_send,
    lat_got,
    stage,
    states32,
    gain32,
    res32,
    part,
    pair_got,
    pair_sum,
    plane_got,
    plane_sum,
    row_got,
    rows,
    xmat,
    small_sem,
    load_sem,
    lat_sem,
    pair_sem,
    plane_sem,
    scatter_sem,
    gather_sem,
    spread_sem,
    share_sem,
):
    group_count, local_count = dims
    n = group_count * local_count
    chips = n // 2
    group = lax.axis_index("group")
    local = lax.axis_index("local")
    me = group * local_count + local
    chip = me // 2
    core = lax.rem(me, 2)
    planes = SLOW if group_count % SLOW == 0 else 1
    plane = chips // planes
    far, near = chip // plane, lax.rem(chip, plane)
    slot = core * chips + near * planes + far
    width = CHUNKS * SEG
    segs = states.shape[1] // width
    tall = stage.shape[0] // n
    heads = queries.shape[1]
    own_heads = uv.shape[0]
    per_head = lat32.shape[0] // heads
    lat_rows = own_heads * per_head
    experts, hidden = gate.shape[0], gate.shape[2]

    def device(index):
        return (index // local_count, lax.rem(index, local_count))

    def same_core(to_far, to_near):
        return device((to_far * plane + to_near) * 2 + core)

    partner = device(chip * 2 + 1 - core)

    first = [
        pltpu.make_async_copy(queries_hbm.at[0], queries, load_sem.at[0]),
        pltpu.make_async_copy(cache_hbm.at[0], cache, load_sem.at[1]),
    ]
    small = [
        pltpu.make_async_copy(source, target, small_sem.at[i])
        for i, (source, target) in enumerate(
            (
                (ids_hbm, ids),
                (scores_hbm, scores),
                (states_hbm, states),
                (gain_hbm, gain),
                (new_hbm, kv_new),
            )
        )
    ]
    for copy in first + small:
        copy.start()
    barrier = pltpu.get_barrier_semaphore()

    def greet(k, carry):
        pl.semaphore_signal(
            barrier, inc=1, device_id=device(lax.rem(me + k, n)), device_id_type=MESH
        )
        return carry

    lax.fori_loop(1, n, greet, 0)

    load_uv = pltpu.make_async_copy(uv_hbm, uv, load_sem.at[2])
    block = wout.shape[0] // PIECES
    load_out = [
        pltpu.make_async_copy(
            out_hbm.at[pl.ds(i * block, block)],
            wout.at[pl.ds(i * block, block)],
            load_sem.at[3 + i],
        )
        for i in range(PIECES)
    ]
    deep = segs * SEG
    load_gate = []
    load_up = []
    load_down = []
    for c in range(CHUNKS):
        for e in range(experts):
            at = 3 + PIECES + (c * experts + e) * 3
            half = pl.ds(c * deep, deep)
            load_gate.append(
                pltpu.make_async_copy(
                    gate_hbm.at[e, half], gate.at[e, half], load_sem.at[at]
                )
            )
            load_up.append(
                pltpu.make_async_copy(up_hbm.at[e, half], up.at[e, half], load_sem.at[at + 1])
            )
            half_rows = hidden // CHUNKS
            load_down.append(
                pltpu.make_async_copy(
                    down_hbm.at[e, pl.ds(c * half_rows, half_rows)],
                    down.at[pl.ds(e * hidden + c * half_rows, half_rows)],
                    load_sem.at[at + 2],
                )
            )

    states32[...] = jnp.zeros_like(states32)
    gain32[...] = jnp.zeros_like(gain32)
    stage[...] = jnp.zeros_like(stage)
    lat32[...] = jnp.zeros_like(lat32)
    for copy in small:
        copy.wait()
    for c in range(CHUNKS):
        for s in range(segs):
            at = (c * segs + s) * SEG
            states32[c, s : s + 1, :] = states[0:1, at : at + SEG].astype(F32)
            gain32[c, s : s + 1, :] = gain[0:1, at : at + SEG]

    lane = lax.broadcasted_iota(jnp.int32, (1, SEG), 1)
    score_sum = scores[0, 0]
    for k in range(1, scores.shape[1]):
        score_sum = score_sum + scores[0, k]
    dense = jnp.zeros((1, SEG), F32)
    for k in range(scores.shape[1]):
        weight = (
            jnp.full((1, SEG), 2.5 * scores[0, k], F32) / jnp.full((1, SEG), score_sum, F32)
        ).astype(BF16).astype(F32)
        dense = dense + jnp.where(lane == ids[0, k], weight, 0.0)

    for copy in first:
        copy.wait()
    for copy in [load_uv] + load_out:
        copy.start()

    scale = (VD + ROPE) ** (-0.5)
    new = kv_new[...].astype(F32)
    cached = (
        lax.dot_general(
            queries[...], cache[...], (((0,), (0,)), ((), ())), preferred_element_type=F32
        )
        * scale
    )
    own = (
        lax.dot_general(
            queries[...], kv_new[...], (((0,), (1,)), ((), ())), preferred_element_type=F32
        )
        * scale
    )
    visible = lax.broadcasted_iota(jnp.int32, cached.shape, 1) < lengths[0]
    cached = jnp.where(visible, cached, -1e30)
    highest = jnp.maximum(jnp.max(cached, axis=1, keepdims=True), own)
    exps = jnp.exp(cached - highest)
    own_exp = jnp.exp(own - highest)
    denominator = jnp.sum(exps, axis=1, keepdims=True) + own_exp
    probs = (exps * (1.0 / denominator)).astype(BF16)
    prob_own = (own_exp / denominator).astype(BF16).astype(F32)
    for i in range(len(load_gate)):
        load_gate[i].start()
        load_up[i].start()
    latent = lax.dot_general(
        cache[:LAT, :], probs, (((1,), (1,)), ((), ())), preferred_element_type=F32
    ).T
    latent = latent + prob_own * new[:, :LAT]
    for q in range(LAT // 128):
        lat32[pl.ds(q, heads, stride=per_head), :] = latent[:, q * 128 : (q + 1) * 128]
    lat_send[...] = lat32[...].astype(BF16).reshape(lat_send.shape)

    pl.semaphore_wait(barrier, n - 1)

    def send_latent(k, carry):
        to = lax.rem(me + k, n)
        pltpu.make_async_remote_copy(
            src_ref=lat_send.at[to],
            dst_ref=lat_got.at[slot],
            send_sem=lat_sem.at[0],
            recv_sem=lat_sem.at[1],
            device_id=device(to),
            device_id_type=MESH,
        ).start()
        return carry

    lax.fori_loop(1, n, send_latent, 0)
    lat_got[pl.ds(slot, 1)] = lat_send[pl.ds(me, 1)]
    for copy in load_down:
        copy.start()
    load_uv.wait()
    others = lat_got.at[pl.ds(0, n - 1)]
    pltpu.make_async_copy(others, others, lat_sem.at[1]).wait()
    lat32[...] = lat_got[...].astype(F32).reshape(lat32.shape)
    values = []
    for h in range(own_heads):
        by_head = jnp.concatenate(
            [
                lat32[pl.ds(h * per_head + q, n, stride=lat_rows), :]
                for q in range(LAT // 128)
            ],
            axis=1,
        ).astype(BF16)
        values.append(jnp.dot(by_head, uv[h], preferred_element_type=F32).astype(BF16))
    values = jnp.concatenate(values, axis=1)

    def scatter_sums(left, weight, turn):
        shares = []

        def multiply(c):
            for s in range(0, segs, WIDE):
                at = (c * segs + s) * SEG
                product = jnp.dot(
                    left, weight[:, at : at + WIDE * SEG], preferred_element_type=F32
                )
                for w in range(WIDE):
                    stage[pl.ds(s + w, n, stride=tall), :] = product[:, w * SEG : (w + 1) * SEG]
            part[turn, c] = stage[...].astype(BF16).reshape(part.shape[2:])
            share = pltpu.make_async_remote_copy(
                src_ref=part.at[turn, c, pl.ds((1 - core) * chips, chips)],
                dst_ref=pair_got.at[turn, c],
                send_sem=pair_sem.at[0, turn, c],
                recv_sem=pair_sem.at[1, turn, c],
                device_id=partner,
                device_id_type=MESH,
            )
            share.start()
            shares.append(share)

        def add_pair(c):
            shares[c].wait()
            pair_sum[turn, c] = (
                (
                    part[turn, c, pl.ds(core * chips, chips)].astype(F32)
                    + pair_got[turn, c].astype(F32)
                )
                .astype(BF16)
                .reshape(pair_sum.shape[2:])
            )
            for k in range(1, plane):
                to = lax.rem(near + k, plane)
                pltpu.make_async_remote_copy(
                    src_ref=pair_sum.at[turn, c, to],
                    dst_ref=plane_got.at[turn, c, near],
                    send_sem=plane_sem.at[0, turn, c],
                    recv_sem=plane_sem.at[1, turn, c],
                    device_id=same_core(far, to),
                    device_id_type=MESH,
                ).start()
            plane_got[turn, c, pl.ds(near, 1)] = pair_sum[turn, c, pl.ds(near, 1)]

        def add_plane(c):
            got = plane_got.at[turn, c, pl.ds(0, plane - 1)]
            pltpu.make_async_copy(got, got, plane_sem.at[1, turn, c]).wait()
            if planes == 1:
                return
            plane_sum[turn, c] = jnp.sum(plane_got[turn, c].astype(F32), axis=0).astype(BF16)
            for k in range(1, planes):
                to = lax.rem(far + k, planes)
                pltpu.make_async_remote_copy(
                    src_ref=plane_sum.at[turn, c, to],
                    dst_ref=row_got.at[turn, c, far],
                    send_sem=scatter_sem.at[0, turn, c],
                    recv_sem=scatter_sem.at[1, turn, c],
                    device_id=same_core(to, near),
                    device_id_type=MESH,
                ).start()
            row_got[turn, c, pl.ds(far, 1)] = plane_sum[turn, c, pl.ds(far, 1)]

        for c in range(CHUNKS + 2):
            if c < CHUNKS:
                multiply(c)
            if 0 <= c - 1 < CHUNKS:
                add_pair(c - 1)
            if 0 <= c - 2:
                add_plane(c - 2)
        sums = []
        for c in range(CHUNKS):
            if planes == 1:
                sums.append(jnp.sum(plane_got[turn, c].astype(F32), axis=0)[0])
                continue
            got = row_got.at[turn, c, pl.ds(0, planes - 1)]
            pltpu.make_async_copy(got, got, scatter_sem.at[1, turn, c]).wait()
            sums.append(jnp.sum(row_got[turn, c].astype(F32), axis=0))
        return sums

    for copy in load_out:
        copy.wait()
    attention = scatter_sums(values, wout, 0)
    square = jnp.zeros((1, 1), F32)
    for c in range(CHUNKS):
        row = (states32[c] + attention[c]).astype(BF16).astype(F32)
        res32[c] = row
        square = square + jnp.sum(
            jnp.sum(row * row, axis=1, keepdims=True), axis=0, keepdims=True
        )
    factor = lax.rsqrt(square / states.shape[1] + 1e-6)
    for c in range(CHUNKS):
        normed = res32[c] * factor * gain32[c]
        if c == 0:
            at_row = lax.broadcasted_iota(jnp.int32, normed.shape, 0)
            normed = jnp.where(at_row == segs, dense, normed)
        rows[c, pl.ds(slot, 1)] = normed.astype(BF16)[None]

        for k in range(1, planes):
            pltpu.make_async_remote_copy(
                src_ref=rows.at[c, slot],
                dst_ref=rows.at[c, slot],
                send_sem=gather_sem.at[0, c],
                recv_sem=gather_sem.at[1, c],
                device_id=same_core(lax.rem(far + k, planes), near),
                device_id_type=MESH,
            ).start()
    shares = []

    def spread(c):
        if planes > 1:
            got = rows.at[c, pl.ds(0, planes - 1)]
            pltpu.make_async_copy(got, got, gather_sem.at[1, c]).wait()
        mine = rows.at[c, pl.ds(core * chips + near * planes, planes)]
        for k in range(1, plane):
            pltpu.make_async_remote_copy(
                src_ref=mine,
                dst_ref=mine,
                send_sem=spread_sem.at[0, c],
                recv_sem=spread_sem.at[1, c],
                device_id=same_core(far, lax.rem(near + k, plane)),
                device_id_type=MESH,
            ).start()

    def hand_over(c):
        got = rows.at[c, pl.ds(0, chips - planes)]
        pltpu.make_async_copy(got, got, spread_sem.at[1, c]).wait()
        mine = rows.at[c, pl.ds(core * chips, chips)]
        share = pltpu.make_async_remote_copy(
            src_ref=mine,
            dst_ref=mine,
            send_sem=share_sem.at[0, c],
            recv_sem=share_sem.at[1, c],
            device_id=partner,
            device_id_type=MESH,
        )
        share.start()
        shares.append(share)

    for c in range(CHUNKS):
        spread(c)
        final[0, c] = res32[c]
    hand_over(0)

    gates = [None] * experts
    ups = [None] * experts
    weights = []
    for c in range(CHUNKS):
        shares[c].wait()
        stage[...] = rows[c].astype(F32).reshape(stage.shape)
        for s in range(segs):
            xmat[:, s * SEG : (s + 1) * SEG] = stage[pl.ds(s, n, stride=tall), :].astype(BF16)
        if c == 0:
            table = stage[pl.ds(segs, n, stride=tall), :]
            lanes = lax.broadcasted_iota(jnp.int32, table.shape, 1)
            for e in range(experts):
                weights.append(
                    jnp.sum(
                        jnp.where(lanes == group * experts + e, table, 0.0),
                        axis=1,
                        keepdims=True,
                    )
                )
        left = xmat[...]
        for e in range(experts):
            if e == 1 and c + 1 < CHUNKS:
                hand_over(c + 1)
            load_gate[c * experts + e].wait()
            load_up[c * experts + e].wait()
            gate_part = jnp.dot(
                left, gate[e, c * deep : (c + 1) * deep, :], preferred_element_type=F32
            )
            up_part = jnp.dot(
                left, up[e, c * deep : (c + 1) * deep, :], preferred_element_type=F32
            )
            gates[e] = gate_part if c == 0 else gates[e] + gate_part
            ups[e] = up_part if c == 0 else ups[e] + up_part
    active = jnp.concatenate(
        [
            (gates[e] / (1.0 + jnp.exp(-gates[e])) * ups[e] * weights[e]).astype(BF16)
            for e in range(experts)
        ],
        axis=1,
    )
    for copy in load_down:
        copy.wait()
    expert_sum = scatter_sums(active, down, 1)
    for c in range(CHUNKS):
        final[1, c] = res32[c] + expert_sum[c]

    sent = lat_send.at[pl.ds(0, n - 1)]
    pltpu.make_async_copy(sent, sent, lat_sem.at[0]).wait()
    for c in range(CHUNKS):
        if planes > 1:
            sent = rows.at[c, pl.ds(0, planes - 1)]
            pltpu.make_async_copy(sent, sent, gather_sem.at[0, c]).wait()
        sent = rows.at[c, pl.ds(0, chips - planes)]
        pltpu.make_async_copy(sent, sent, spread_sem.at[0, c]).wait()
        for turn in range(2):
            sent = pair_sum.at[turn, c, pl.ds(0, plane - 1)]
            pltpu.make_async_copy(sent, sent, plane_sem.at[0, turn, c]).wait()
            if planes > 1:
                sent = plane_sum.at[turn, c, pl.ds(0, planes - 1)]
                pltpu.make_async_copy(sent, sent, scatter_sem.at[0, turn, c]).wait()


def write_rows(final, residual_out, layer_out):
    segs = residual_out.shape[1] // (CHUNKS * SEG)
    for which, out in enumerate((residual_out, layer_out)):
        for c in range(CHUNKS):
            for s in range(segs):
                at = (c * segs + s) * SEG
                out[0:1, at : at + SEG] = final[which, c, s : s + 1, :].astype(BF16)


def body(
    group_count,
    local_count,
    states_in,
    queries,
    kv_cache,
    kv_new,
    lengths,
    w_uv,
    w_out,
    norm_gain,
    expert_ids,
    route_scores,
    w_gate,
    w_up,
    w_down,
):
    n = group_count * local_count
    chips = n // 2
    d = states_in.shape[1]
    heads, q_width = queries.shape[1:]
    cache_len = kv_cache.shape[1]
    planes = SLOW if group_count % SLOW == 0 else 1
    plane = chips // planes
    own_heads = w_uv.shape[0]
    experts, _, hidden = w_gate.shape
    segs = d // (CHUNKS * SEG)
    tall = -(-(segs + 1) // TILE) * TILE
    per_head = max(LAT // 128, TILE // own_heads)
    lat_rows = own_heads * per_head
    smem = pl.BlockSpec(memory_space=pltpu.SMEM)
    vmem = pl.BlockSpec(memory_space=pltpu.VMEM)
    hbm = pl.BlockSpec(memory_space=pl.ANY)
    row = jax.ShapeDtypeStruct((1, d), BF16)
    final = pl.pallas_call(
        functools.partial(kernel, (group_count, local_count)),
        out_shape=jax.ShapeDtypeStruct((2, CHUNKS, tall, SEG), F32),
        in_specs=[smem] + [hbm] * 12,
        out_specs=vmem,
        scratch_shapes=[
            pltpu.SMEM(expert_ids.shape, jnp.int32),
            pltpu.SMEM(route_scores.shape, F32),
            pltpu.VMEM((1, d), BF16),
            pltpu.VMEM((1, d), F32),
            pltpu.VMEM(kv_new.shape, BF16),
            pltpu.VMEM((q_width, heads), BF16),
            pltpu.VMEM((q_width, cache_len), BF16),
            pltpu.VMEM(w_uv.shape, BF16),
            pltpu.VMEM(w_out.shape, BF16),
            pltpu.VMEM(w_gate.shape, BF16),
            pltpu.VMEM(w_up.shape, BF16),
            pltpu.VMEM((experts * hidden, d), BF16),
            pltpu.VMEM((heads * per_head, 128), F32),
            pltpu.VMEM((n, lat_rows, 128), BF16),
            pltpu.VMEM((n, lat_rows, 128), BF16),
            pltpu.VMEM((n * tall, SEG), F32),
            pltpu.VMEM((CHUNKS, tall, SEG), F32),
            pltpu.VMEM((CHUNKS, tall, SEG), F32),
            pltpu.VMEM((CHUNKS, tall, SEG), F32),
            pltpu.VMEM((2, CHUNKS, n, tall, SEG), BF16),
            pltpu.VMEM((2, CHUNKS, chips, tall, SEG), BF16),
            pltpu.VMEM((2, CHUNKS, plane, planes, tall, SEG), BF16),
            pltpu.VMEM((2, CHUNKS, plane, planes, tall, SEG), BF16),
            pltpu.VMEM((2, CHUNKS, planes, tall, SEG), BF16),
            pltpu.VMEM((2, CHUNKS, planes, tall, SEG), BF16),
            pltpu.VMEM((CHUNKS, n, tall, SEG), BF16),
            pltpu.VMEM((n, segs * SEG), BF16),
            pltpu.SemaphoreType.DMA((5,)),
            pltpu.SemaphoreType.DMA((3 + PIECES + 3 * CHUNKS * experts,)),
            pltpu.SemaphoreType.DMA((2,)),
            pltpu.SemaphoreType.DMA((2, 2, CHUNKS)),
            pltpu.SemaphoreType.DMA((2, 2, CHUNKS)),
            pltpu.SemaphoreType.DMA((2, 2, CHUNKS)),
            pltpu.SemaphoreType.DMA((2, CHUNKS)),
            pltpu.SemaphoreType.DMA((2, CHUNKS)),
            pltpu.SemaphoreType.DMA((2, CHUNKS)),
        ],
        compiler_params=pltpu.CompilerParams(
            collective_id=0, has_side_effects=True, vmem_limit_bytes=60 * 1024 * 1024
        ),
    )(
        lengths,
        expert_ids,
        route_scores,
        states_in,
        norm_gain.reshape(1, d),
        kv_new,
        jnp.swapaxes(queries, 1, 2),
        jnp.swapaxes(kv_cache, 1, 2),
        w_uv,
        w_out,
        w_gate,
        w_up,
        w_down,
    )
    return pl.pallas_call(
        write_rows, out_shape=(row, row), in_specs=[vmem], out_specs=(vmem, vmem)
    )(final)


def solution(mesh):
    in_specs = (
        P(("group", "local"), None),
        P(("group", "local"), None, None),
        P(("group", "local"), None, None),
        P(("group", "local"), None),
        P(("group", "local")),
        P(("group", "local"), None, None),
        P(("group", "local"), None),
        P(),
        P(("group", "local"), None),
        P(("group", "local"), None),
        P("group", None, "local"),
        P("group", None, "local"),
        P("group", "local", None),
    )
    out_specs = (P(("group", "local"), None), P(("group", "local"), None))
    sizes = (mesh.shape["group"], mesh.shape["local"])
    return jax.shard_map(
        functools.partial(body, *sizes),
        mesh=mesh,
        in_specs=in_specs,
        out_specs=out_specs,
        check_vma=False,
    )
```

```python
import functools

import jax
import jax.numpy as jnp
from jax import lax
from jax.experimental import pallas as pl
from jax.experimental.pallas import tpu as pltpu
from jax.sharding import PartitionSpec as P

LAT = 512
ROPE = 64
VD = 128
CHUNKS = 2
SEG = 128
WIDE = 2
TILE = 16
PIECES = 4
SLOW = 1
MESH = pl.DeviceIdType.MESH
F32 = jnp.float32
BF16 = jnp.bfloat16


def far_first(count):
    return sorted(range(1, count), key=lambda k: abs(k - count // 2))


def kernel(
    dims,
    lengths,
    ids_hbm,
    scores_hbm,
    states_hbm,
    gain_hbm,
    new_hbm,
    queries_hbm,
    cache_hbm,
    uv_hbm,
    out_hbm,
    gate_hbm,
    up_hbm,
    down_hbm,
    final,
    ids,
    scores,
    states,
    gain,
    kv_new,
    queries,
    cache,
    uv,
    wout,
    gate,
    up,
    down,
    lat32,
    lat_send,
    lat_got,
    stage,
    states32,
    gain32,
    res32,
    part,
    pair_got,
    pair_sum,
    plane_got,
    plane_sum,
    row_got,
    rows,
    xmat,
    small_sem,
    load_sem,
    lat_sem,
    pair_sem,
    plane_sem,
    scatter_sem,
    gather_sem,
    spread_sem,
    share_sem,
):
    group_count, local_count = dims
    n = group_count * local_count
    chips = n // 2
    group = lax.axis_index("group")
    local = lax.axis_index("local")
    me = group * local_count + local
    chip = me // 2
    core = lax.rem(me, 2)
    planes = SLOW if group_count % SLOW == 0 else 1
    plane = chips // planes
    far, near = chip // plane, lax.rem(chip, plane)
    slot = core * chips + near * planes + far
    width = CHUNKS * SEG
    segs = states.shape[1] // width
    tall = stage.shape[0] // n
    heads = queries.shape[1]
    own_heads = uv.shape[0]
    per_head = lat32.shape[0] // heads
    lat_rows = own_heads * per_head
    experts, hidden = gate.shape[0], gate.shape[2]

    def device(index):
        return (index // local_count, lax.rem(index, local_count))

    def same_core(to_far, to_near):
        return device((to_far * plane + to_near) * 2 + core)

    partner = device(chip * 2 + 1 - core)

    first = [
        pltpu.make_async_copy(queries_hbm.at[0], queries, load_sem.at[0]),
        pltpu.make_async_copy(cache_hbm.at[0], cache, load_sem.at[1]),
    ]
    small = [
        pltpu.make_async_copy(source, target, small_sem.at[i])
        for i, (source, target) in enumerate(
            (
                (ids_hbm, ids),
                (scores_hbm, scores),
                (states_hbm, states),
                (gain_hbm, gain),
                (new_hbm, kv_new),
            )
        )
    ]
    for copy in first + small:
        copy.start()
    barrier = pltpu.get_barrier_semaphore()

    def greet(k, carry):
        pl.semaphore_signal(
            barrier, inc=1, device_id=device(lax.rem(me + k, n)), device_id_type=MESH
        )
        return carry

    lax.fori_loop(1, n, greet, 0)

    load_uv = pltpu.make_async_copy(uv_hbm, uv, load_sem.at[2])
    block = wout.shape[0] // PIECES
    load_out = [
        pltpu.make_async_copy(
            out_hbm.at[pl.ds(i * block, block)],
            wout.at[pl.ds(i * block, block)],
            load_sem.at[3 + i],
        )
        for i in range(PIECES)
    ]
    deep = segs * SEG
    load_gate = []
    load_up = []
    load_down = []
    for c in range(CHUNKS):
        for e in range(experts):
            at = 3 + PIECES + (c * experts + e) * 3
            half = pl.ds(c * deep, deep)
            load_gate.append(
                pltpu.make_async_copy(
                    gate_hbm.at[e, half], gate.at[e, half], load_sem.at[at]
                )
            )
            load_up.append(
                pltpu.make_async_copy(up_hbm.at[e, half], up.at[e, half], load_sem.at[at + 1])
            )
            half_rows = hidden // CHUNKS
            load_down.append(
                pltpu.make_async_copy(
                    down_hbm.at[e, pl.ds(c * half_rows, half_rows)],
                    down.at[pl.ds(e * hidden + c * half_rows, half_rows)],
                    load_sem.at[at + 2],
                )
            )

    states32[...] = jnp.zeros_like(states32)
    gain32[...] = jnp.zeros_like(gain32)
    stage[...] = jnp.zeros_like(stage)
    lat32[...] = jnp.zeros_like(lat32)
    for copy in small:
        copy.wait()
    for c in range(CHUNKS):
        for s in range(segs):
            at = (c * segs + s) * SEG
            states32[c, s : s + 1, :] = states[0:1, at : at + SEG].astype(F32)
            gain32[c, s : s + 1, :] = gain[0:1, at : at + SEG]

    lane = lax.broadcasted_iota(jnp.int32, (1, SEG), 1)
    score_sum = scores[0, 0]
    for k in range(1, scores.shape[1]):
        score_sum = score_sum + scores[0, k]
    dense = jnp.zeros((1, SEG), F32)
    for k in range(scores.shape[1]):
        weight = (
            jnp.full((1, SEG), 2.5 * scores[0, k], F32) / jnp.full((1, SEG), score_sum, F32)
        ).astype(BF16).astype(F32)
        dense = dense + jnp.where(lane == ids[0, k], weight, 0.0)

    for copy in first:
        copy.wait()
    for copy in [load_uv] + load_out:
        copy.start()

    scale = (VD + ROPE) ** (-0.5)
    new = kv_new[...].astype(F32)
    cached = (
        lax.dot_general(
            queries[...], cache[...], (((0,), (0,)), ((), ())), preferred_element_type=F32
        )
        * scale
    )
    own = (
        lax.dot_general(
            queries[...], kv_new[...], (((0,), (1,)), ((), ())), preferred_element_type=F32
        )
        * scale
    )
    visible = lax.broadcasted_iota(jnp.int32, cached.shape, 1) < lengths[0]
    cached = jnp.where(visible, cached, -1e30)
    highest = jnp.maximum(jnp.max(cached, axis=1, keepdims=True), own)
    exps = jnp.exp(cached - highest)
    own_exp = jnp.exp(own - highest)
    denominator = jnp.sum(exps, axis=1, keepdims=True) + own_exp
    probs = (exps * (1.0 / denominator)).astype(BF16)
    prob_own = (own_exp / denominator).astype(BF16).astype(F32)
    latent = lax.dot_general(
        cache[:LAT, :], probs, (((1,), (1,)), ((), ())), preferred_element_type=F32
    ).T
    latent = latent + prob_own * new[:, :LAT]
    for q in range(LAT // 128):
        lat32[pl.ds(q, heads, stride=per_head), :] = latent[:, q * 128 : (q + 1) * 128]
    lat_send[...] = lat32[...].astype(BF16).reshape(lat_send.shape)

    pl.semaphore_wait(barrier, n - 1)

    def send_latent(k, carry):
        to = lax.rem(me + n // 2 + (1 - 2 * lax.rem(k, 2)) * ((k + 1) // 2), n)
        pltpu.make_async_remote_copy(
            src_ref=lat_send.at[to],
            dst_ref=lat_got.at[slot],
            send_sem=lat_sem.at[0],
            recv_sem=lat_sem.at[1],
            device_id=device(to),
            device_id_type=MESH,
        ).start()
        return carry

    lax.fori_loop(0, n - 1, send_latent, 0)
    lat_got[pl.ds(slot, 1)] = lat_send[pl.ds(me, 1)]
    for i in range(len(load_gate)):
        load_gate[i].start()
        load_up[i].start()
    for copy in load_down:
        copy.start()
    load_uv.wait()
    others = lat_got.at[pl.ds(0, n - 1)]
    pltpu.make_async_copy(others, others, lat_sem.at[1]).wait()
    lat32[...] = lat_got[...].astype(F32).reshape(lat32.shape)
    values = []
    for h in range(own_heads):
        by_head = jnp.concatenate(
            [
                lat32[pl.ds(h * per_head + q, n, stride=lat_rows), :]
                for q in range(LAT // 128)
            ],
            axis=1,
        ).astype(BF16)
        values.append(jnp.dot(by_head, uv[h], preferred_element_type=F32).astype(BF16))
    values = jnp.concatenate(values, axis=1)

    def scatter_sums(left, weight, turn):
        shares = []

        def multiply(c):
            for s in range(0, segs, WIDE):
                at = (c * segs + s) * SEG
                product = jnp.dot(
                    left, weight[:, at : at + WIDE * SEG], preferred_element_type=F32
                )
                for w in range(WIDE):
                    stage[pl.ds(s + w, n, stride=tall), :] = product[:, w * SEG : (w + 1) * SEG]
            part[turn, c] = stage[...].astype(BF16).reshape(part.shape[2:])
            share = pltpu.make_async_remote_copy(
                src_ref=part.at[turn, c, pl.ds((1 - core) * chips, chips)],
                dst_ref=pair_got.at[turn, c],
                send_sem=pair_sem.at[0, turn, c],
                recv_sem=pair_sem.at[1, turn, c],
                device_id=partner,
                device_id_type=MESH,
            )
            share.start()
            shares.append(share)

        def add_pair(c):
            shares[c].wait()
            pair_sum[turn, c] = (
                (
                    part[turn, c, pl.ds(core * chips, chips)].astype(F32)
                    + pair_got[turn, c].astype(F32)
                )
                .astype(BF16)
                .reshape(pair_sum.shape[2:])
            )
            for k in far_first(plane):
                to = lax.rem(near + k, plane)
                pltpu.make_async_remote_copy(
                    src_ref=pair_sum.at[turn, c, to],
                    dst_ref=plane_got.at[turn, c, near],
                    send_sem=plane_sem.at[0, turn, c],
                    recv_sem=plane_sem.at[1, turn, c],
                    device_id=same_core(far, to),
                    device_id_type=MESH,
                ).start()
            plane_got[turn, c, pl.ds(near, 1)] = pair_sum[turn, c, pl.ds(near, 1)]

        def add_plane(c):
            got = plane_got.at[turn, c, pl.ds(0, plane - 1)]
            pltpu.make_async_copy(got, got, plane_sem.at[1, turn, c]).wait()
            if planes == 1:
                return
            plane_sum[turn, c] = jnp.sum(plane_got[turn, c].astype(F32), axis=0).astype(BF16)
            for k in far_first(planes):
                to = lax.rem(far + k, planes)
                pltpu.make_async_remote_copy(
                    src_ref=plane_sum.at[turn, c, to],
                    dst_ref=row_got.at[turn, c, far],
                    send_sem=scatter_sem.at[0, turn, c],
                    recv_sem=scatter_sem.at[1, turn, c],
                    device_id=same_core(to, near),
                    device_id_type=MESH,
                ).start()
            row_got[turn, c, pl.ds(far, 1)] = plane_sum[turn, c, pl.ds(far, 1)]

        for c in range(CHUNKS + 2):
            if c < CHUNKS:
                multiply(c)
            if 0 <= c - 1 < CHUNKS:
                add_pair(c - 1)
            if 0 <= c - 2:
                add_plane(c - 2)
        sums = []
        for c in range(CHUNKS):
            if planes == 1:
                sums.append(jnp.sum(plane_got[turn, c].astype(F32), axis=0)[0])
                continue
            got = row_got.at[turn, c, pl.ds(0, planes - 1)]
            pltpu.make_async_copy(got, got, scatter_sem.at[1, turn, c]).wait()
            sums.append(jnp.sum(row_got[turn, c].astype(F32), axis=0))
        return sums

    for copy in load_out:
        copy.wait()
    attention = scatter_sums(values, wout, 0)
    square = jnp.zeros((1, 1), F32)
    for c in range(CHUNKS):
        row = (states32[c] + attention[c]).astype(BF16).astype(F32)
        res32[c] = row
        square = square + jnp.sum(
            jnp.sum(row * row, axis=1, keepdims=True), axis=0, keepdims=True
        )
    factor = lax.rsqrt(square / states.shape[1] + 1e-6)
    for c in range(CHUNKS):
        normed = res32[c] * factor * gain32[c]
        if c == 0:
            at_row = lax.broadcasted_iota(jnp.int32, normed.shape, 0)
            normed = jnp.where(at_row == segs, dense, normed)
        rows[c, pl.ds(slot, 1)] = normed.astype(BF16)[None]

        for k in far_first(planes):
            pltpu.make_async_remote_copy(
                src_ref=rows.at[c, slot],
                dst_ref=rows.at[c, slot],
                send_sem=gather_sem.at[0, c],
                recv_sem=gather_sem.at[1, c],
                device_id=same_core(lax.rem(far + k, planes), near),
                device_id_type=MESH,
            ).start()
    shares = []

    def spread(c):
        if planes > 1:
            got = rows.at[c, pl.ds(0, planes - 1)]
            pltpu.make_async_copy(got, got, gather_sem.at[1, c]).wait()
        mine = rows.at[c, pl.ds(core * chips + near * planes, planes)]
        for k in far_first(plane):
            pltpu.make_async_remote_copy(
                src_ref=mine,
                dst_ref=mine,
                send_sem=spread_sem.at[0, c],
                recv_sem=spread_sem.at[1, c],
                device_id=same_core(far, lax.rem(near + k, plane)),
                device_id_type=MESH,
            ).start()

    def hand_over(c):
        got = rows.at[c, pl.ds(0, chips - planes)]
        pltpu.make_async_copy(got, got, spread_sem.at[1, c]).wait()
        mine = rows.at[c, pl.ds(core * chips, chips)]
        share = pltpu.make_async_remote_copy(
            src_ref=mine,
            dst_ref=mine,
            send_sem=share_sem.at[0, c],
            recv_sem=share_sem.at[1, c],
            device_id=partner,
            device_id_type=MESH,
        )
        share.start()
        shares.append(share)

    for c in range(CHUNKS):
        spread(c)
        final[0, c] = res32[c]
    hand_over(0)

    gates = [None] * experts
    ups = [None] * experts
    weights = []
    for c in range(CHUNKS):
        shares[c].wait()
        stage[...] = rows[c].astype(F32).reshape(stage.shape)
        for s in range(segs):
            xmat[:, s * SEG : (s + 1) * SEG] = stage[pl.ds(s, n, stride=tall), :].astype(BF16)
        if c == 0:
            table = stage[pl.ds(segs, n, stride=tall), :]
            lanes = lax.broadcasted_iota(jnp.int32, table.shape, 1)
            for e in range(experts):
                weights.append(
                    jnp.sum(
                        jnp.where(lanes == group * experts + e, table, 0.0),
                        axis=1,
                        keepdims=True,
                    )
                )
        left = xmat[...]
        for e in range(experts):
            if e == 1 and c + 1 < CHUNKS:
                hand_over(c + 1)
            load_gate[c * experts + e].wait()
            load_up[c * experts + e].wait()
            gate_part = jnp.dot(
                left, gate[e, c * deep : (c + 1) * deep, :], preferred_element_type=F32
            )
            up_part = jnp.dot(
                left, up[e, c * deep : (c + 1) * deep, :], preferred_element_type=F32
            )
            gates[e] = gate_part if c == 0 else gates[e] + gate_part
            ups[e] = up_part if c == 0 else ups[e] + up_part
    active = jnp.concatenate(
        [
            (gates[e] / (1.0 + jnp.exp(-gates[e])) * ups[e] * weights[e]).astype(BF16)
            for e in range(experts)
        ],
        axis=1,
    )
    for copy in load_down:
        copy.wait()
    expert_sum = scatter_sums(active, down, 1)
    for c in range(CHUNKS):
        final[1, c] = res32[c] + expert_sum[c]

    sent = lat_send.at[pl.ds(0, n - 1)]
    pltpu.make_async_copy(sent, sent, lat_sem.at[0]).wait()
    for c in range(CHUNKS):
        if planes > 1:
            sent = rows.at[c, pl.ds(0, planes - 1)]
            pltpu.make_async_copy(sent, sent, gather_sem.at[0, c]).wait()
        sent = rows.at[c, pl.ds(0, chips - planes)]
        pltpu.make_async_copy(sent, sent, spread_sem.at[0, c]).wait()
        for turn in range(2):
            sent = pair_sum.at[turn, c, pl.ds(0, plane - 1)]
            pltpu.make_async_copy(sent, sent, plane_sem.at[0, turn, c]).wait()
            if planes > 1:
                sent = plane_sum.at[turn, c, pl.ds(0, planes - 1)]
                pltpu.make_async_copy(sent, sent, scatter_sem.at[0, turn, c]).wait()


def write_rows(final, residual_out, layer_out):
    segs = residual_out.shape[1] // (CHUNKS * SEG)
    for which, out in enumerate((residual_out, layer_out)):
        for c in range(CHUNKS):
            for s in range(segs):
                at = (c * segs + s) * SEG
                out[0:1, at : at + SEG] = final[which, c, s : s + 1, :].astype(BF16)


def body(
    group_count,
    local_count,
    states_in,
    queries,
    kv_cache,
    kv_new,
    lengths,
    w_uv,
    w_out,
    norm_gain,
    expert_ids,
    route_scores,
    w_gate,
    w_up,
    w_down,
):
    n = group_count * local_count
    chips = n // 2
    d = states_in.shape[1]
    heads, q_width = queries.shape[1:]
    cache_len = kv_cache.shape[1]
    planes = SLOW if group_count % SLOW == 0 else 1
    plane = chips // planes
    own_heads = w_uv.shape[0]
    experts, _, hidden = w_gate.shape
    segs = d // (CHUNKS * SEG)
    tall = -(-(segs + 1) // TILE) * TILE
    per_head = max(LAT // 128, TILE // own_heads)
    lat_rows = own_heads * per_head
    smem = pl.BlockSpec(memory_space=pltpu.SMEM)
    vmem = pl.BlockSpec(memory_space=pltpu.VMEM)
    hbm = pl.BlockSpec(memory_space=pl.ANY)
    row = jax.ShapeDtypeStruct((1, d), BF16)
    final = pl.pallas_call(
        functools.partial(kernel, (group_count, local_count)),
        out_shape=jax.ShapeDtypeStruct((2, CHUNKS, tall, SEG), F32),
        in_specs=[smem] + [hbm] * 12,
        out_specs=vmem,
        scratch_shapes=[
            pltpu.SMEM(expert_ids.shape, jnp.int32),
            pltpu.SMEM(route_scores.shape, F32),
            pltpu.VMEM((1, d), BF16),
            pltpu.VMEM((1, d), F32),
            pltpu.VMEM(kv_new.shape, BF16),
            pltpu.VMEM((q_width, heads), BF16),
            pltpu.VMEM((q_width, cache_len), BF16),
            pltpu.VMEM(w_uv.shape, BF16),
            pltpu.VMEM(w_out.shape, BF16),
            pltpu.VMEM(w_gate.shape, BF16),
            pltpu.VMEM(w_up.shape, BF16),
            pltpu.VMEM((experts * hidden, d), BF16),
            pltpu.VMEM((heads * per_head, 128), F32),
            pltpu.VMEM((n, lat_rows, 128), BF16),
            pltpu.VMEM((n, lat_rows, 128), BF16),
            pltpu.VMEM((n * tall, SEG), F32),
            pltpu.VMEM((CHUNKS, tall, SEG), F32),
            pltpu.VMEM((CHUNKS, tall, SEG), F32),
            pltpu.VMEM((CHUNKS, tall, SEG), F32),
            pltpu.VMEM((2, CHUNKS, n, tall, SEG), BF16),
            pltpu.VMEM((2, CHUNKS, chips, tall, SEG), BF16),
            pltpu.VMEM((2, CHUNKS, plane, planes, tall, SEG), BF16),
            pltpu.VMEM((2, CHUNKS, plane, planes, tall, SEG), BF16),
            pltpu.VMEM((2, CHUNKS, planes, tall, SEG), BF16),
            pltpu.VMEM((2, CHUNKS, planes, tall, SEG), BF16),
            pltpu.VMEM((CHUNKS, n, tall, SEG), BF16),
            pltpu.VMEM((n, segs * SEG), BF16),
            pltpu.SemaphoreType.DMA((5,)),
            pltpu.SemaphoreType.DMA((3 + PIECES + 3 * CHUNKS * experts,)),
            pltpu.SemaphoreType.DMA((2,)),
            pltpu.SemaphoreType.DMA((2, 2, CHUNKS)),
            pltpu.SemaphoreType.DMA((2, 2, CHUNKS)),
            pltpu.SemaphoreType.DMA((2, 2, CHUNKS)),
            pltpu.SemaphoreType.DMA((2, CHUNKS)),
            pltpu.SemaphoreType.DMA((2, CHUNKS)),
            pltpu.SemaphoreType.DMA((2, CHUNKS)),
        ],
        compiler_params=pltpu.CompilerParams(
            collective_id=0, has_side_effects=True, vmem_limit_bytes=60 * 1024 * 1024
        ),
    )(
        lengths,
        expert_ids,
        route_scores,
        states_in,
        norm_gain.reshape(1, d),
        kv_new,
        jnp.swapaxes(queries, 1, 2),
        jnp.swapaxes(kv_cache, 1, 2),
        w_uv,
        w_out,
        w_gate,
        w_up,
        w_down,
    )
    return pl.pallas_call(
        write_rows, out_shape=(row, row), in_specs=[vmem], out_specs=(vmem, vmem)
    )(final)


def solution(mesh):
    in_specs = (
        P(("group", "local"), None),
        P(("group", "local"), None, None),
        P(("group", "local"), None, None),
        P(("group", "local"), None),
        P(("group", "local")),
        P(("group", "local"), None, None),
        P(("group", "local"), None),
        P(),
        P(("group", "local"), None),
        P(("group", "local"), None),
        P("group", None, "local"),
        P("group", None, "local"),
        P("group", "local", None),
    )
    out_specs = (P(("group", "local"), None), P(("group", "local"), None))
    sizes = (mesh.shape["group"], mesh.shape["local"])
    return jax.shard_map(
        functools.partial(body, *sizes),
        mesh=mesh,
        in_specs=in_specs,
        out_specs=out_specs,
        check_vma=False,
    )
```
